256 devices in a mesh: tm: 64 (over y, z, x_hi), fsdp: 4 (over x_lo, core).
Axes of the slice: x: 4 (x_hi: 2, x_lo: 2; x = x_hi * 2 + x_lo), y: 4, z: 8, core: 2. Of those that a mesh axis runs over, the one named last changes fastest.
Arguments:
- frames_in: bfloat16 [8, 8192, 1536], P('fsdp', 'tm'), may hold values from -24 to 24
- lengths: int32 [8], replicated, may hold values from 2048 to 8192, as said below
- depth_kernel: float32 [32, 1536], replicated, may hold values from -1 to 1
- norm_gain: float32 [1536], replicated, may hold values from 0.1 to 1.9
- norm_bias: float32 [1536], replicated, may hold values from -3 to 3
- out_weight: bfloat16 [1536, 1536], P(None, 'fsdp'), may hold values from -0.15625 to 0.15625
- cotangent: bfloat16 [8, 8192, 1536], P('fsdp', 'tm'), may hold values from -16 to 16
Outputs:
- mixed: bfloat16 [8, 8192, 1536], P('fsdp', 'tm')
- frames_grad: bfloat16 [8, 8192, 1536], P('fsdp', 'tm')
- weight_grad: float32 [1536, 1536], P(None, 'fsdp')
- kernel_grad: float32 [32, 1536], replicated
- gain_grad: float32 [1536], replicated
- bias_grad: float32 [1536], replicated
The draws below stay inside these ranges and needn't reach their ends.
Inputs may be any that keep to these rules, and one draw needn't show every extreme that they name: `lengths`: one utterance has exactly 8192 valid frames.
All inputs are finite; a program needn't handle non-finite values.
Results may differ from the reference program's by a relative error of at most 0.005.
Values may be sent and summed in bfloat16 or wider, within the bound.
No kernel may reach another device: no remote copies, remote signals or barrier semaphores. Data moves between devices by JAX's collectives and lax.ppermute only.
A program may use at most 128 MiB of HBM per device.

```python
import math
import jax
import jax.numpy as jnp
from jax import lax

D = 1536
KT = 32
FRAMES = 8192
UTTS = 8


def draw_frames_in(key, part):
    key = jax.random.fold_in(key, 3)
    key_base, key_chan, key_offset = jax.random.split(key, 3)
    positions = jnp.arange(FRAMES, dtype=jnp.float32) / FRAMES
    rising = (0.5 + 1.5 * positions)[None, :, None]
    channel_scale = jnp.exp(jax.random.uniform(key_chan, (1, 1, D), jnp.float32, math.log(0.3), math.log(3.0)))
    offset = 0.5 * jax.random.normal(key_offset, (1, 1, D), jnp.float32)
    base = jnp.clip(jax.random.normal(key_base, (UTTS, FRAMES, D), jnp.float32), -6.0, 6.0)
    values = jnp.clip(rising * channel_scale * base + offset, -24.0, 24.0)
    return values.astype(jnp.bfloat16)


def draw_lengths(key, part):
    key = jax.random.fold_in(key, 7)
    key_base, key_pick = jax.random.split(key)
    drawn = jax.random.randint(key_base, (UTTS,), FRAMES // 4, FRAMES + 1)
    chosen = jax.random.randint(key_pick, (), 0, UTTS)
    indices = jnp.arange(UTTS, dtype=jnp.int32)
    drawn = jnp.where(indices == chosen, FRAMES, drawn)
    return drawn.astype(jnp.int32)


def raised(entries, key, source, target, shards_of, factor):
    owner, partner = [(jnp.arange(entries.shape[axis_at]) // (entries.shape[axis_at] // shards_of)).reshape([-1 if axis == axis_at else 1 for axis in range(entries.ndim)]) for axis_at in (source, target)]
    chosen = jax.random.permutation(key, shards_of)[partner]
    strong = (owner == chosen) | (owner == (partner + shards_of // 2) % shards_of)
    return jnp.where(strong, factor * entries, entries)


def levels(stream_key, dims, shards, low, high):
    factor_of = 1.0
    for position, blocks in shards:
        steps = jax.random.uniform(jax.random.fold_in(jax.random.fold_in(stream_key, 6), position), (blocks,), jnp.float32, low / len(shards), high / len(shards))
        factor_of = factor_of * jnp.repeat(jnp.exp(steps), dims[position] // blocks).reshape((-1,) + (1,) * (len(dims) - 1 - position))
    return factor_of


def gaussian(stream_key, shape, spread, limit, pieces=(), held_as=jnp.bfloat16):
    result = spread * jax.random.normal(stream_key, shape, jnp.float32)
    if pieces:
        result = result * levels(stream_key, shape, pieces, -0.22, 0.18)
    return jnp.clip(result, -limit, limit).astype(held_as)


def heavy_noise(key, dims, spread, bound, cuts, heavy, held_as=jnp.bfloat16):
    array = spread * jax.random.normal(key, dims, jnp.float32)
    if cuts:
        array = array * levels(key, dims, cuts, -0.22, 0.18)
    return jnp.clip(raised(array, jax.random.fold_in(key, 3), *heavy), -bound, bound).astype(held_as)


def setup_inputs(seed: int = 0) -> dict:
    seeds = jax.random.split(jax.random.key(seed), 8)
    return {
        "frames_in": draw_frames_in(jax.random.fold_in(seeds[7], 71), 0),
        "lengths": draw_lengths(jax.random.fold_in(seeds[7], 71), 0),
        "depth_kernel": gaussian(seeds[2], (KT, D), KT ** -0.5, 1.0, (), jnp.float32),
        "norm_gain": jnp.clip(1.0 + 0.18 * jax.random.normal(seeds[3], (D,), jnp.float32), 0.1, 1.9),
        "norm_bias": gaussian(seeds[4], (D,), 0.5, 3.0, (), jnp.float32),
        "out_weight": gaussian(seeds[5], (D, D), D ** -0.5, 0.15625, ((1, 4),)),
        "cotangent": heavy_noise(seeds[6], (UTTS, FRAMES, D), 1.0, 16.0, ((0, 4), (1, 64)), (1, 2, 64, 4.0)),
    }


epsilon = 1e-05

def depthwise(sequence, kernel):
    total_rows = sequence.shape[0]
    padded = jnp.concatenate([jnp.zeros((KT - 1, sequence.shape[1]), jnp.float32), sequence], 0)

    def add_tap(tap_index, running):
        window = lax.dynamic_slice_in_dim(padded, tap_index, total_rows, 0)
        return running + kernel[tap_index] * window
    return lax.fori_loop(0, KT, add_tap, jnp.zeros(sequence.shape, jnp.float32))

def reference(frames_in, lengths, depth_kernel, norm_gain, norm_bias, out_weight, cotangent):
    positions = jnp.arange(FRAMES, dtype=jnp.int32)
    valid = (positions[None, :] < lengths[:, None]).astype(jnp.float32)
    frames_valid = jnp.sum(lengths).astype(jnp.float32)
    masked = frames_in.astype(jnp.float32) * valid[:, :, None]

    def channel_total(item):
        sequence, rows_on = item
        return lax.optimization_barrier(jnp.sum(depthwise(sequence, depth_kernel) * rows_on[:, None], axis=0))
    average = lax.optimization_barrier(jnp.sum(lax.map(channel_total, (masked, valid)), axis=0)) / frames_valid

    def channel_square(item):
        sequence, rows_on = item
        centred = depthwise(sequence, depth_kernel) - average
        return lax.optimization_barrier(jnp.sum(centred * centred * rows_on[:, None], axis=0))
    variance = lax.optimization_barrier(jnp.sum(lax.map(channel_square, (masked, valid)), axis=0)) / frames_valid
    inv_spread = lax.rsqrt(variance + epsilon)

    def forward_one(item):
        sequence, rows_on, grad_rows = item
        normed = (depthwise(sequence, depth_kernel) - average) * inv_spread
        preact = normed * norm_gain + norm_bias
        active = jax.nn.silu(preact).astype(jnp.bfloat16)
        mixed = (jnp.dot(active, out_weight, preferred_element_type=jnp.float32) * rows_on[:, None]).astype(jnp.bfloat16)
        masked_grad = (grad_rows.astype(jnp.float32) * rows_on[:, None]).astype(jnp.bfloat16)
        weight_term = lax.dot_general(active, masked_grad, (((0,), (0,)), ((), ())), preferred_element_type=jnp.float32)
        act_grad = lax.dot_general(masked_grad, out_weight, (((1,), (1,)), ((), ())), preferred_element_type=jnp.float32)
        sigmoid_pre = jax.nn.sigmoid(preact)
        pre_grad = act_grad * sigmoid_pre * (1.0 + preact * (1.0 - sigmoid_pre))
        bias_part = lax.optimization_barrier(jnp.sum(pre_grad * rows_on[:, None], axis=0))
        gain_part = lax.optimization_barrier(jnp.sum(pre_grad * normed * rows_on[:, None], axis=0))
        return (mixed, weight_term, pre_grad, bias_part, gain_part)
    mixed, weight_terms, pre_grads, bias_parts, gain_parts = lax.map(forward_one, (masked, valid, cotangent))
    weight_grad = lax.optimization_barrier(jnp.sum(weight_terms, axis=0))
    bias_grad = lax.optimization_barrier(jnp.sum(bias_parts, axis=0))
    gain_grad = lax.optimization_barrier(jnp.sum(gain_parts, axis=0))

    def backward_one(item):
        sequence, rows_on, pre_grad = item
        normed = (depthwise(sequence, depth_kernel) - average) * inv_spread
        conv_grad = rows_on[:, None] * norm_gain * inv_spread * (pre_grad - bias_grad / frames_valid - normed * gain_grad / frames_valid)
        padded = jnp.concatenate([jnp.zeros((KT - 1, D), jnp.float32), sequence], 0)
        kernel_part = jnp.stack([lax.optimization_barrier(jnp.sum(padded[tap_index:tap_index + FRAMES] * conv_grad, axis=0)) for tap_index in range(KT)])
        extended = jnp.concatenate([conv_grad, jnp.zeros((KT - 1, D), jnp.float32)], 0)

        def add_tap(tap_index, running):
            window = lax.dynamic_slice_in_dim(extended, KT - 1 - tap_index, FRAMES, 0)
            return running + depth_kernel[tap_index] * window
        backed = lax.fori_loop(0, KT, add_tap, jnp.zeros((FRAMES, D), jnp.float32))
        return ((backed * rows_on[:, None]).astype(jnp.bfloat16), kernel_part)
    frames_grad, kernel_parts = lax.map(backward_one, (masked, valid, pre_grads))
    kernel_grad = lax.optimization_barrier(jnp.sum(kernel_parts, axis=0))
    return (mixed, frames_grad, weight_grad, kernel_grad, gain_grad, bias_grad)
```

```python
import functools
import jax
import jax.numpy as jnp
from jax import lax
from jax.experimental import pallas as pl
from jax.experimental.pallas import tpu as pltpu
from jax.sharding import PartitionSpec as P

epsilon = 1e-05
LANES = 128
HALO = 32
f32, bf16 = jnp.float32, jnp.bfloat16


def masked_rows(value, first, limit):
    rows = first + lax.broadcasted_iota(jnp.int32, value.shape, 0)
    return jnp.where(rows < limit, value.astype(f32), 0.0)


def conv_kernel(limits, taps, before, own, convolved, stats, padded):
    utts, rows = own.shape[0], own.shape[1]
    total = jnp.zeros((1, LANES), f32)
    valid_count = 0.0
    for utt in range(utts):
        limit = limits[utt]
        padded[utt, 0:HALO, :] = masked_rows(before[utt], -HALO, limit)
        padded[utt, HALO : HALO + rows, :] = masked_rows(own[utt], 0, limit)
        for start in range(0, rows, 64):
            result = jnp.zeros((64, LANES), f32)
            for tap in range(HALO):
                result = result + taps[tap : tap + 1, :] * padded[utt, start + tap + 1 : start + tap + 65, :]
            convolved[utt, start : start + 64, :] = result
            total = total + jnp.sum(masked_rows(result, start, limit), axis=0, keepdims=True)
        valid_count = valid_count + jnp.clip(limit, 0, rows).astype(f32)
    mean = total / jnp.maximum(valid_count, 1.0)
    squares = jnp.zeros((1, LANES), f32)
    for utt in range(utts):
        centred = masked_rows(convolved[utt] - mean, 0, limits[utt])
        squares = squares + jnp.sum(centred * centred, axis=0, keepdims=True)
    stats[0:1, :] = total
    stats[1:2, :] = squares


def depthwise(limits, taps, before, own):
    utts, rows, channels = own.shape
    tiles = channels // LANES
    return pl.pallas_call(
        conv_kernel,
        grid_spec=pltpu.PrefetchScalarGridSpec(
            num_scalar_prefetch=1,
            grid=(tiles,),
            in_specs=[
                pl.BlockSpec((HALO, LANES), lambda j, s: (0, j)),
                pl.BlockSpec((utts, HALO, LANES), lambda j, s: (0, 0, j)),
                pl.BlockSpec((utts, rows, LANES), lambda j, s: (0, 0, j)),
            ],
            out_specs=[
                pl.BlockSpec((utts, rows, LANES), lambda j, s: (0, 0, j)),
                pl.BlockSpec((2, LANES), lambda j, s: (0, j)),
            ],
            scratch_shapes=[pltpu.VMEM((utts, HALO + rows, LANES), f32)],
        ),
        out_shape=[
            jax.ShapeDtypeStruct(own.shape, f32),
            jax.ShapeDtypeStruct((2, channels), f32),
        ],
        compiler_params=pltpu.CompilerParams(vmem_limit_bytes=24 << 20),
        cost_estimate=pl.CostEstimate(flops=30_000_000, bytes_accessed=3_000_000, transcendentals=0),
    )(limits, taps, before, own)


def project_kernel(scalars, convolved, params, cotangent, active_out, grad_out, send, keep, active):
    utts, rows, channels = convolved.shape
    step = pl.program_id(0)

    @pl.when(step == 0)
    def _():
        for utt in range(utts):
            for start in range(0, rows, 32):
                normed = (convolved[utt, start : start + 32, :] - params[0:1, :]) * params[1:2, :]
                preact = normed * params[2:3, :] + params[3:4, :]
                value = jax.nn.silu(preact).astype(bf16)
                at = utt * rows + start
                active[at : at + 32, :] = value
                active_out[at : at + 32, :] = value

    block = cotangent.shape[2]
    parts = []
    for utt in range(utts):
        parts.append(masked_rows(cotangent[utt], 0, scalars[utt]).astype(bf16))
    masked = jnp.concatenate(parts, 0)
    grad_out[...] = masked
    for start in range(0, channels, 384):
        term = lax.dot_general(
            active[:, start : start + 384], masked, (((0,), (0,)), ((), ())), preferred_element_type=f32
        )

        @pl.when(step < 2)
        def _():
            send[0, start : start + 384, :] = term.astype(bf16)

        @pl.when(step >= 2)
        def _():
            keep[0, start : start + 384, :] = term


def project(scalars, convolved, params, cotangent):
    utts, rows, channels = convolved.shape
    block = channels // 4
    whole = utts * rows
    return pl.pallas_call(
        project_kernel,
        grid_spec=pltpu.PrefetchScalarGridSpec(
            num_scalar_prefetch=1,
            grid=(4,),
            in_specs=[
                pl.BlockSpec((utts, rows, channels), lambda j, s: (0, 0, 0)),
                pl.BlockSpec((4, channels), lambda j, s: (0, 0)),
                pl.BlockSpec((utts, rows, block), lambda j, s: (0, 0, s[2 + j])),
            ],
            out_specs=[
                pl.BlockSpec((whole, channels), lambda j, s: (0, 0)),
                pl.BlockSpec((whole, block), lambda j, s: (0, s[2 + j])),
                pl.BlockSpec((1, channels, block), lambda j, s: (jnp.minimum(j, 1), 0, 0)),
                pl.BlockSpec((1, channels, block), lambda j, s: (jnp.maximum(j - 2, 0), 0, 0)),
            ],
            scratch_shapes=[pltpu.VMEM((whole, channels), bf16)],
        ),
        out_shape=[
            jax.ShapeDtypeStruct((whole, channels), bf16),
            jax.ShapeDtypeStruct((whole, channels), bf16),
            jax.ShapeDtypeStruct((2, channels, block), bf16),
            jax.ShapeDtypeStruct((2, channels, block), f32),
        ],
        compiler_params=pltpu.CompilerParams(vmem_limit_bytes=32 << 20),
        cost_estimate=pl.CostEstimate(
            flops=2 * whole * channels * channels, bytes_accessed=12_000_000, transcendentals=whole * channels
        ),
    )(scalars, convolved, params, cotangent)


def sums_kernel(
    scalars, taps, params, before, own, after, convolved, act_grad, sums, pre_out, normed_out, padded, pre, norm
):
    utts, rows = own.shape[0], own.shape[1]
    reach = rows + HALO
    mean, inverse, gain, shift = (params[i : i + 1, :] for i in range(4))
    bias_sum = jnp.zeros((1, LANES), f32)
    gain_sum = jnp.zeros((1, LANES), f32)
    ones = jnp.zeros((HALO, LANES), f32)
    for utt in range(utts):
        limit = scalars[utt]
        padded[utt, 0:HALO, :] = masked_rows(before[utt], -HALO, limit)
        padded[utt, HALO : HALO + rows, :] = masked_rows(own[utt], 0, limit)
        padded[utt, HALO + rows :, :] = masked_rows(after[utt], rows, limit)
        beyond = jnp.zeros((HALO, LANES), f32)
        for tap in range(HALO):
            beyond = beyond + taps[tap : tap + 1, :] * padded[utt, rows + tap + 1 : rows + tap + 1 + HALO, :]
        for start in range(0, reach, 32):
            value = convolved[utt, start : start + 32, :] if start < rows else beyond
            normed = (value - mean) * inverse
            preact = normed * gain + shift
            sigmoid = jax.nn.sigmoid(preact)
            grad = act_grad[utt, start : start + 32, :] * sigmoid * (1.0 + preact * (1.0 - sigmoid))
            grad = masked_rows(grad, start, limit)
            normed = masked_rows(normed, start, limit)
            pre[utt, start : start + 32, :] = grad
            norm[utt, start : start + 32, :] = normed
            pre_out[utt, start : start + 32, :] = grad
            normed_out[utt, start : start + 32, :] = normed
            if start < rows:
                bias_sum = bias_sum + jnp.sum(grad, axis=0, keepdims=True)
                gain_sum = gain_sum + jnp.sum(grad * normed, axis=0, keepdims=True)
        lag = (
            lax.broadcasted_iota(jnp.int32, (HALO, reach), 1)
            - lax.broadcasted_iota(jnp.int32, (HALO, reach), 0)
            - 1
        )
        band = jnp.where((lag >= 0) & (lag < jnp.minimum(limit, rows)), 1.0, 0.0).astype(bf16)
        ones = ones + jnp.dot(band, padded[utt, 0:reach, :].astype(bf16), preferred_element_type=f32)
    for first in range(0, HALO, 8):
        by_pre = [jnp.zeros((8, LANES), f32) for _ in range(8)]
        by_norm = [jnp.zeros((8, LANES), f32) for _ in range(8)]
        for utt in range(utts):
            for row in range(0, rows, 8):
                grad = pre[utt, row : row + 8, :]
                normed = norm[utt, row : row + 8, :]
                for tap in range(8):
                    at = row + first + tap + 1
                    window = padded[utt, at : at + 8, :]
                    by_pre[tap] = by_pre[tap] + window * grad
                    by_norm[tap] = by_norm[tap] + window * normed
        for tap in range(8):
            sums[0, first + tap : first + tap + 1, :] = jnp.sum(by_pre[tap], axis=0, keepdims=True)
            sums[0, 64 + first + tap : 65 + first + tap, :] = jnp.sum(by_norm[tap], axis=0, keepdims=True)
    sums[0, 32:64, :] = ones
    sums[0, 96:128, :] = jnp.zeros((32, LANES), f32)
    sums[0, 96:97, :] = bias_sum
    sums[0, 97:98, :] = gain_sum


def channel_sums(scalars, taps, params, before, own, after, convolved, act_grad):
    utts, rows, channels = own.shape
    reach = rows + HALO
    block_tiles = channels // 4 // LANES

    def slot(j, s):
        place = s[6 + j // block_tiles]
        return (place, 0, j % block_tiles)

    by_tile = lambda j, s: (0, 0, j)
    return pl.pallas_call(
        sums_kernel,
        grid_spec=pltpu.PrefetchScalarGridSpec(
            num_scalar_prefetch=1,
            grid=(channels // LANES,),
            in_specs=[
                pl.BlockSpec((HALO, LANES), lambda j, s: (0, j)),
                pl.BlockSpec((4, LANES), lambda j, s: (0, j)),
                pl.BlockSpec((utts, HALO, LANES), by_tile),
                pl.BlockSpec((utts, rows, LANES), by_tile),
                pl.BlockSpec((utts, HALO, LANES), by_tile),
                pl.BlockSpec((utts, rows, LANES), by_tile),
                pl.BlockSpec((utts, reach, LANES), by_tile),
            ],
            out_specs=[
                pl.BlockSpec((1, 128, LANES), slot),
                pl.BlockSpec((utts, reach, LANES), by_tile),
                pl.BlockSpec((utts, reach, LANES), by_tile),
            ],
            scratch_shapes=[
                pltpu.VMEM((utts, HALO + reach, LANES), f32),
                pltpu.VMEM((utts, reach, LANES), f32),
                pltpu.VMEM((utts, reach, LANES), f32),
            ],
        ),
        out_shape=[
            jax.ShapeDtypeStruct((4, 128, channels // 4), f32),
            jax.ShapeDtypeStruct((utts, reach, channels), f32),
            jax.ShapeDtypeStruct((utts, reach, channels), f32),
        ],
        compiler_params=pltpu.CompilerParams(vmem_limit_bytes=24 << 20),
        cost_estimate=pl.CostEstimate(flops=80_000_000, bytes_accessed=12_000_000, transcendentals=500_000),
    )(scalars, taps, params, before, own, after, convolved, act_grad)


def back_kernel(limits, taps, params, pre, normed, out, grad):
    utts, rows = out.shape[0], out.shape[1]
    scale, bias_mean, gain_mean = (params[i : i + 1, :] for i in range(3))
    for utt in range(utts):
        limit = limits[utt]
        value = pre[utt] - bias_mean - normed[utt] * gain_mean
        grad[utt] = masked_rows(value * scale, 0, limit)
        for start in range(0, rows, 64):
            result = jnp.zeros((64, LANES), f32)
            for ahead in range(HALO):
                tap = HALO - 1 - ahead
                result = result + taps[tap : tap + 1, :] * grad[utt, start + ahead : start + ahead + 64, :]
            out[utt, start : start + 64, :] = masked_rows(result, start, limit).astype(bf16)


def frames_back(limits, taps, params, pre, normed, rows):
    utts, reach, channels = pre.shape
    by_tile = lambda j, s: (0, 0, j)
    return pl.pallas_call(
        back_kernel,
        grid_spec=pltpu.PrefetchScalarGridSpec(
            num_scalar_prefetch=1,
            grid=(channels // LANES,),
            in_specs=[
                pl.BlockSpec((HALO, LANES), lambda j, s: (0, j)),
                pl.BlockSpec((3, LANES), lambda j, s: (0, j)),
                pl.BlockSpec((utts, reach, LANES), by_tile),
                pl.BlockSpec((utts, reach, LANES), by_tile),
            ],
            out_specs=pl.BlockSpec((utts, rows, LANES), by_tile),
            scratch_shapes=[pltpu.VMEM((utts, reach, LANES), f32)],
        ),
        out_shape=jax.ShapeDtypeStruct((utts, rows, channels), bf16),
        compiler_params=pltpu.CompilerParams(vmem_limit_bytes=24 << 20),
        cost_estimate=pl.CostEstimate(flops=30_000_000, bytes_accessed=5_000_000, transcendentals=0),
    )(limits, taps, params, pre, normed)


def moved(value, steps):
    count = lax.axis_size("tm")
    return lax.ppermute(value, "tm", [(i, i + steps) for i in range(count) if 0 <= i + steps < count])


def other_core(value):
    return lax.ppermute(value, "fsdp", [(0, 1), (1, 0), (2, 3), (3, 2)])


def other_chip(value):
    return lax.ppermute(value, "fsdp", [(0, 2), (2, 0), (1, 3), (3, 1)])


def merged(total, squares, counts):
    count = jnp.sum(counts, axis=0)
    sum_all = jnp.sum(total, axis=0)
    mean = sum_all / jnp.maximum(count, 1.0)
    apart = total / jnp.maximum(counts, 1.0) - mean
    return sum_all, mean, jnp.sum(squares + counts * apart * apart, axis=0), count


def in_three(value):
    first = lax.reduce_precision(value, 8, 7)
    second = lax.reduce_precision(value - first, 8, 7)
    third = value - first - second
    return first.astype(bf16), second.astype(bf16), third.astype(bf16)


def on_device(frames_in, lengths, depth_kernel, norm_gain, norm_bias, out_weight, cotangent):
    utts, rows, channels = frames_in.shape
    tm, fsdp = lax.axis_index("tm"), lax.axis_index("fsdp")
    tm_count, fsdp_count = lax.axis_size("tm"), lax.axis_size("fsdp")
    block = channels // fsdp_count
    chip, core = fsdp // 2, fsdp % 2
    frames_valid = jnp.sum(lengths).astype(f32)
    own_lengths = lax.dynamic_slice_in_dim(lengths, fsdp * utts, utts, 0)
    limits = own_lengths - tm * rows
    near, far = chip * 2, (1 - chip) * 2
    order = jnp.stack([near + 1 - core, far + 1 - core, near + core, far + core])
    index = jnp.arange(4, dtype=jnp.int32)
    place = jnp.where(index % 2 == core, 0, 2) + jnp.where(index // 2 == chip, 0, 1)
    scalars = jnp.concatenate([limits, order, place]).astype(jnp.int32)

    whole_weight = lax.all_gather(out_weight, "fsdp", axis=1, tiled=True)
    before = moved(frames_in[:, rows - HALO :, :], 1)
    before, ahead_frames, ahead_grads = lax.optimization_barrier(
        (before, frames_in[:, :HALO, :], cotangent[:, :HALO, :])
    )
    ahead = moved(jnp.concatenate([ahead_frames, ahead_grads], 0), -1)
    after, after_grad = ahead[:utts], ahead[utts:]

    convolved, stats = depthwise(scalars, depth_kernel, before, frames_in)

    by_fsdp = lax.all_gather(stats, "fsdp")
    mine = lax.dynamic_slice_in_dim(by_fsdp, fsdp * block, block, 2)
    at_tm = jnp.clip(lengths[None, :] - rows * jnp.arange(tm_count, dtype=jnp.int32)[:, None], 0, rows)
    here = jnp.clip(lengths - tm * rows, 0, rows).reshape(fsdp_count, utts).sum(1).astype(f32)
    total, _, squares, _ = merged(mine[:, 0], mine[:, 1], here[:, None])
    third = block // LANES
    piece = jnp.concatenate(
        [total.reshape(third, LANES), squares.reshape(third, LANES), jnp.zeros((8 - 2 * third, LANES), f32)], 0
    )
    pieces = lax.all_to_all(jnp.broadcast_to(piece, (tm_count, 8, LANES)), "tm", 0, 0, tiled=True)
    counts = jnp.sum(at_tm, axis=1).astype(f32)[:, None, None]
    _, mean, squares, _ = merged(pieces[:, :third], pieces[:, third : 2 * third], counts)
    inverse = lax.rsqrt(squares / frames_valid + epsilon)
    norm_params = lax.all_gather(jnp.stack([mean.reshape(block), inverse.reshape(block)]), "fsdp")
    norm_params = norm_params.transpose(1, 0, 2).reshape(2, channels)
    params = jnp.concatenate([norm_params, norm_gain[None], norm_bias[None]], 0)

    active, masked_grad, send, keep = project(scalars, convolved, params, cotangent)
    arrived = other_core(send)
    far_sum = (keep[1] + arrived[1].astype(f32)).astype(bf16)
    far_arrived = other_chip(far_sum)

    ahead_valid = (rows + jnp.arange(HALO, dtype=jnp.int32))[None, :] < limits[:, None]
    after_grad = jnp.where(ahead_valid[:, :, None], after_grad, jnp.zeros((), bf16))
    reach_grad = jnp.concatenate([masked_grad.reshape(utts, rows, channels), after_grad], 1)
    act_grad = lax.dot_general(
        reach_grad.reshape(utts * (rows + HALO), channels),
        whole_weight,
        (((1,), (1,)), ((), ())),
        preferred_element_type=f32,
    ).reshape(utts, rows + HALO, channels)
    sums, pre, normed = channel_sums(
        scalars, depth_kernel, params, before, frames_in, after, convolved, act_grad
    )
    sums_near = sums[:2] + other_core(sums[2:])
    own_sums = sums_near[0] + other_chip(sums_near[1])

    valid_rows = jnp.arange(rows, dtype=jnp.int32)[None, :] < limits[:, None]
    projected = jnp.dot(active, whole_weight, preferred_element_type=f32).reshape(utts, rows, channels)
    mixed = jnp.where(valid_rows[:, :, None], projected, 0.0).astype(bf16)

    own_weight = keep[0] + arrived[0].astype(f32) + far_arrived.astype(f32)
    weight_rows = channels // tm_count
    sum_rows = own_sums.shape[0] // tm_count
    spare = jnp.zeros((tm_count, 8 - 3 * sum_rows, block), bf16)
    split = [part.reshape(tm_count, sum_rows, block) for part in in_three(own_sums)]
    outgoing = jnp.concatenate([own_weight.astype(bf16).reshape(tm_count, weight_rows, block), *split, spare], 1)
    incoming = lax.all_to_all(outgoing, "tm", 0, 0, tiled=True)
    summed = jnp.sum(incoming.astype(f32), axis=0)
    parts = summed[weight_rows : weight_rows + 3 * sum_rows].reshape(3, sum_rows, block)
    reduced = parts[0] + parts[1] + parts[2]
    piece = jnp.concatenate(
        [summed[:weight_rows].astype(bf16), *in_three(reduced), jnp.zeros((8 - 3 * sum_rows, block), bf16)], 0
    )
    gathered = lax.all_to_all(
        jnp.broadcast_to(piece, (tm_count, *piece.shape)), "tm", 0, 0, tiled=True
    )
    weight_grad = gathered[:, :weight_rows].astype(f32).reshape(channels, block)
    terms = gathered[:, weight_rows : weight_rows + 3 * sum_rows].astype(f32).reshape(tm_count, 3, sum_rows, block)
    all_sums = (terms[:, 0] + terms[:, 1] + terms[:, 2]).reshape(tm_count * sum_rows, block)
    bias_own, gain_own = all_sums[96], all_sums[97]
    inverse_own = inverse.reshape(block)
    gain_scale = lax.dynamic_slice_in_dim(norm_gain, fsdp * block, block, 0) * inverse_own
    kernel_own = gain_scale * (
        all_sums[0:32] - bias_own / frames_valid * all_sums[32:64] - gain_own / frames_valid * all_sums[64:96]
    )
    final = jnp.concatenate([kernel_own, all_sums[96:98], jnp.zeros((6, block), f32)], 0)
    final = lax.all_gather(final, "fsdp", axis=1, tiled=True)
    kernel_grad, bias_grad, gain_grad = final[:32], final[32], final[33]
    back_params = jnp.stack([norm_gain * params[1], bias_grad / frames_valid, gain_grad / frames_valid])
    frames_grad = frames_back(scalars, depth_kernel, back_params, pre, normed, rows)
    return (mixed, frames_grad, weight_grad, kernel_grad, gain_grad, bias_grad)


def solution(mesh):
    in_specs = (P("fsdp", "tm", None), P(), P(), P(), P(), P(None, "fsdp"), P("fsdp", "tm", None))
    out_specs = (P("fsdp", "tm", None), P("fsdp", "tm", None), P(None, "fsdp"), P(), P(), P())
    return jax.shard_map(
        on_device, mesh=mesh, in_specs=in_specs, out_specs=out_specs, check_vma=False
    )
```

```python
import functools
import jax
import jax.numpy as jnp
from jax import lax
from jax.experimental import pallas as pl
from jax.experimental.pallas import tpu as pltpu
from jax.sharding import PartitionSpec as P

epsilon = 1e-05
LANES = 128
HALO = 32
f32, bf16 = jnp.float32, jnp.bfloat16


def masked_rows(value, first, limit):
    rows = first + lax.broadcasted_iota(jnp.int32, value.shape, 0)
    return jnp.where(rows < limit, value.astype(f32), 0.0)


def limit_of(place, utt, utts, rows):
    return place[place[9] * utts + utt] - place[8] * rows


def chip_of(place):
    return (place[8] & 1) * 2 + (place[9] >> 1)


def conv_kernel(place, taps, before, own, convolved, stats, padded):
    utts, rows = own.shape[0], own.shape[1]
    total = jnp.zeros((1, LANES), f32)
    valid_count = 0.0
    for utt in range(utts):
        limit = limit_of(place, utt, utts, rows)
        padded[utt, 0:HALO, :] = masked_rows(before[utt], -HALO, limit)
        padded[utt, HALO : HALO + rows, :] = masked_rows(own[utt], 0, limit)
        for start in range(0, rows, 64):
            result = jnp.zeros((64, LANES), f32)
            for tap in range(HALO):
                result = result + taps[tap : tap + 1, :] * padded[utt, start + tap + 1 : start + tap + 65, :]
            convolved[utt, start : start + 64, :] = result
            total = total + jnp.sum(masked_rows(result, start, limit), axis=0, keepdims=True)
        valid_count = valid_count + jnp.clip(limit, 0, rows).astype(f32)
    mean = total / jnp.maximum(valid_count, 1.0)
    squares = jnp.zeros((1, LANES), f32)
    for utt in range(utts):
        centred = masked_rows(convolved[utt] - mean, 0, limit_of(place, utt, utts, rows))
        squares = squares + jnp.sum(centred * centred, axis=0, keepdims=True)
    stats[0, 0:1, :] = total
    stats[0, 1:2, :] = squares
    stats[0, 2:3, :] = jnp.zeros((1, LANES), f32) + valid_count


def stats_place(tiles):
    def index(j, s):
        column = j // tiles
        return ((column ^ s[9]) & 1, 0, (column >> 1) * tiles + j % tiles)

    return index


def merge_rows(parts):
    count = sum(part[2:3, :] for part in parts)
    total = sum(part[0:1, :] for part in parts)
    mean = total / jnp.maximum(count, 1.0)
    squares = jnp.zeros_like(mean)
    for part in parts:
        apart = part[0:1, :] / jnp.maximum(part[2:3, :], 1.0) - mean
        squares = squares + part[1:2, :] + part[2:3, :] * apart * apart
    return total, squares, count


def pair_kernel(own, got, out):
    total, squares, count = merge_rows([own[0], got[...]])
    out[0:1, :] = total
    out[1:2, :] = squares
    out[2:3, :] = count


def ring_kernel(own, first, second, third, out):
    total, squares, count = merge_rows([own[...], first[...], second[...], third[...]])
    tiles = total.shape[1] // LANES
    rows = [value[:, i * LANES : (i + 1) * LANES] for value in (total, squares) for i in range(tiles)]
    rows += [count[:, 0:LANES]] * (out.shape[1] - 2 * tiles)
    out[...] = jnp.broadcast_to(jnp.concatenate(rows, 0)[None], out.shape)


def moments_kernel(lengths, pieces, out):
    tiles = out.shape[1] // LANES
    total, squares = pieces[:, 0:tiles, :], pieces[:, tiles : 2 * tiles, :]
    counts = pieces[:, 2 * tiles : 2 * tiles + 1, :]
    valid = lengths[0]
    for utt in range(1, lengths.shape[0]):
        valid = valid + lengths[utt]
    mean = jnp.sum(total, axis=0) / jnp.sum(counts, axis=0)
    apart = total / jnp.maximum(counts, 1.0) - mean[None]
    variance = jnp.sum(squares + counts * apart * apart, axis=0) / (jnp.zeros_like(mean) + valid.astype(f32))
    inverse = lax.rsqrt(variance + epsilon)
    for i in range(tiles):
        out[0:1, i * LANES : (i + 1) * LANES] = mean[i : i + 1, :]
        out[1:2, i * LANES : (i + 1) * LANES] = inverse[i : i + 1, :]


def params_kernel(place, mine, theirs, gain, shift, out):
    block = gain.shape[1] // 4
    core = place[9] & 1
    for chip in range(2):
        part = slice(chip * block, (chip + 1) * block)
        first = pl.multiple_of(chip * 2 * block + core * block, LANES)
        second = pl.multiple_of(chip * 2 * block + (1 - core) * block, LANES)
        out[0:2, pl.ds(first, block)] = mine[:, part]
        out[0:2, pl.ds(second, block)] = theirs[:, part]
    out[2:3, :] = gain[...]
    out[3:4, :] = shift[...]


def in_vmem(kernel, shape, *operands, scalars=0):
    smem, vmem = pl.BlockSpec(memory_space=pltpu.SMEM), pl.BlockSpec(memory_space=pltpu.VMEM)
    return pl.pallas_call(
        kernel,
        in_specs=[smem] * scalars + [vmem] * (len(operands) - scalars),
        out_specs=vmem,
        out_shape=jax.ShapeDtypeStruct(shape, f32),
        compiler_params=pltpu.CompilerParams(vmem_limit_bytes=16 << 20),
        cost_estimate=pl.CostEstimate(flops=100_000, bytes_accessed=50_000, transcendentals=0),
    )(*operands)


def depthwise(place, taps, before, own):
    utts, rows, channels = own.shape
    tiles = channels // LANES
    return pl.pallas_call(
        conv_kernel,
        grid_spec=pltpu.PrefetchScalarGridSpec(
            num_scalar_prefetch=1,
            grid=(tiles,),
            in_specs=[
                pl.BlockSpec((HALO, LANES), lambda j, s: (0, j)),
                pl.BlockSpec((utts, HALO, LANES), lambda j, s: (0, 0, j)),
                pl.BlockSpec((utts, rows, LANES), lambda j, s: (0, 0, j)),
            ],
            out_specs=[
                pl.BlockSpec((utts, rows, LANES), lambda j, s: (0, 0, j)),
                pl.BlockSpec((1, 3, LANES), stats_place(tiles // 4)),
            ],
            scratch_shapes=[pltpu.VMEM((utts, HALO + rows, LANES), f32)],
        ),
        out_shape=[
            jax.ShapeDtypeStruct(own.shape, f32),
            jax.ShapeDtypeStruct((2, 3, channels // 2), f32),
        ],
        compiler_params=pltpu.CompilerParams(vmem_limit_bytes=24 << 20),
        cost_estimate=pl.CostEstimate(flops=30_000_000, bytes_accessed=3_000_000, transcendentals=0),
    )(place, taps, before, own)


QUARTERS = ((2, 0), (1, 1), (2, 1), (3, 0), (1, 0), (3, 1), (0, 0), (0, 1))


def quarter_term(place, active, grads, quarter):
    size = active.shape[1] // 4
    side, row = place[10 + quarter], place[18 + quarter]
    first = pl.multiple_of(((chip_of(place) + side & 3) >> 1) * (2 * size) + row * size, LANES)
    masked = jnp.concatenate([grads[utt] for utt in range(grads.shape[0])], 0)
    return lax.dot_general(
        active[:, pl.ds(first, size)], masked, (((0,), (0,)), ((), ())), preferred_element_type=f32
    )


def send_kernel(place, convolved, params, grads_even, grads_odd, active_out, first, rest, active):
    utts, rows, channels = convolved.shape
    step = pl.program_id(0)

    @pl.when(step == 0)
    def _():
        for utt in range(utts):
            limit = limit_of(place, utt, utts, rows)
            for start in range(0, rows, 32):
                normed = (convolved[utt, start : start + 32, :] - params[0:1, :]) * params[1:2, :]
                preact = normed * params[2:3, :] + params[3:4, :]
                value = masked_rows(jax.nn.silu(preact), start, limit).astype(bf16)
                at = utt * rows + start
                active[at : at + 32, :] = value
                active_out[at : at + 32, :] = value

    even = quarter_term(place, active, grads_even, 2 * step).astype(bf16)
    odd = quarter_term(place, active, grads_odd, 2 * step + 1).astype(bf16)

    @pl.when(step < 2)
    def _():
        first[0] = even
        first[1] = odd

    @pl.when(step >= 2)
    def _():
        rest[0] = even
        rest[1] = odd


def keep_kernel(place, active, grads_even, grads_odd, first, rest):
    step = pl.program_id(0)
    even = quarter_term(place, active, grads_even, 2 * step)
    odd = quarter_term(place, active, grads_odd, 2 * step + 1)

    @pl.when(step < 2)
    def _():
        first[0] = even
        first[1] = odd

    @pl.when(step >= 2)
    def _():
        rest[0] = even
        rest[1] = odd


def weight_terms(place, convolved, params, reach_grad):
    utts, rows, channels = convolved.shape
    block = channels // 4
    whole = utts * rows

    def column(odd, other):
        return lambda i, s: (
            0,
            0,
            (chip_of(s) + s[10 + 2 * i + odd] & 1) * 2 + ((s[9] & 1) ^ other),
        )

    early = lambda i, s: (jnp.minimum(i, 1), 0, 0)
    late = lambda i, s: (jnp.maximum(i - 2, 0), 0, 0)
    active, send_first, send_rest = pl.pallas_call(
        send_kernel,
        grid_spec=pltpu.PrefetchScalarGridSpec(
            num_scalar_prefetch=1,
            grid=(4,),
            in_specs=[
                pl.BlockSpec((utts, rows, channels), lambda i, s: (0, 0, 0)),
                pl.BlockSpec((4, channels), lambda i, s: (0, 0)),
                pl.BlockSpec((utts, rows, block), column(0, 1)),
                pl.BlockSpec((utts, rows, block), column(1, 1)),
            ],
            out_specs=[
                pl.BlockSpec((whole, channels), lambda i, s: (0, 0)),
                pl.BlockSpec((2, block, block), early),
                pl.BlockSpec((2, block, block), late),
            ],
            scratch_shapes=[pltpu.VMEM((whole, channels), bf16)],
        ),
        out_shape=[
            jax.ShapeDtypeStruct((whole, channels), bf16),
            jax.ShapeDtypeStruct((4, block, block), bf16),
            jax.ShapeDtypeStruct((4, block, block), bf16),
        ],
        compiler_params=pltpu.CompilerParams(vmem_limit_bytes=24 << 20),
        cost_estimate=pl.CostEstimate(
            flops=whole * channels * channels, bytes_accessed=6_000_000, transcendentals=whole * channels
        ),
    )(place, convolved, params, reach_grad, reach_grad)
    keep_first, keep_rest = pl.pallas_call(
        keep_kernel,
        grid_spec=pltpu.PrefetchScalarGridSpec(
            num_scalar_prefetch=1,
            grid=(4,),
            in_specs=[
                pl.BlockSpec((whole, channels), lambda i, s: (0, 0)),
                pl.BlockSpec((utts, rows, block), column(0, 0)),
                pl.BlockSpec((utts, rows, block), column(1, 0)),
            ],
            out_specs=[
                pl.BlockSpec((2, block, block), early),
                pl.BlockSpec((2, block, block), late),
            ],
        ),
        out_shape=[jax.ShapeDtypeStruct((4, block, block), f32)] * 2,
        compiler_params=pltpu.CompilerParams(vmem_limit_bytes=24 << 20),
        cost_estimate=pl.CostEstimate(
            flops=whole * channels * channels, bytes_accessed=6_000_000, transcendentals=0
        ),
    )(place, active, reach_grad, reach_grad)
    return active, send_first, send_rest, keep_first, keep_rest


def pack_kernel(base, low, high, sums, out):
    groups, size = out.shape[0], out.shape[1] - 8
    first = pl.program_id(0) * groups
    total = base[...] + jnp.where(pl.program_id(0) < 2, low[...].astype(f32), high[...].astype(f32))
    filler = jnp.zeros((2, total.shape[1]), f32)
    for group in range(groups):
        row = first + group
        ride = jnp.concatenate([sums[pl.ds(row, 1), :], sums[pl.ds(32 + row, 1), :], sums[64:65, :]], 0)
        rounded = ride.astype(bf16).astype(f32)
        out[group] = jnp.concatenate(
            [total[group * size : (group + 1) * size], rounded, ride - rounded, filler], 0
        ).astype(bf16)


def packed(base, low, high, sums, count):
    half, block = base.shape
    size = half // count
    groups = count // 4
    by_rows = lambda i: (i, 0)
    return pl.pallas_call(
        pack_kernel,
        grid=(count // groups,),
        in_specs=[
            pl.BlockSpec((groups * size, block), by_rows),
            pl.BlockSpec((groups * size, block), lambda i: (jnp.minimum(i, 1), 0)),
            pl.BlockSpec((groups * size, block), lambda i: (jnp.maximum(i - 2, 0), 0)),
            pl.BlockSpec(sums.shape, lambda i: (0, 0)),
        ],
        out_specs=pl.BlockSpec((groups, size + 8, block), lambda i: (i, 0, 0)),
        out_shape=jax.ShapeDtypeStruct((count, size + 8, block), bf16),
        compiler_params=pltpu.CompilerParams(vmem_limit_bytes=16 << 20),
        cost_estimate=pl.CostEstimate(flops=2_000_000, bytes_accessed=4_000_000, transcendentals=0),
    )(base, low, high, sums)


def fill_padded(place, padded, before, own, after):
    utts, rows = own.shape[0], own.shape[1]
    for utt in range(utts):
        limit = limit_of(place, utt, utts, rows)
        padded[utt, 0:HALO, :] = masked_rows(before[utt], -HALO, limit)
        padded[utt, HALO : HALO + rows, :] = masked_rows(own[utt], 0, limit)
        if after is not None:
            padded[utt, HALO + rows :, :] = masked_rows(after[utt], rows, limit)


def correlate(padded, other, rows, store):
    for first in range(0, HALO, 8):
        running = [jnp.zeros((8, LANES), f32) for _ in range(8)]
        for utt in range(padded.shape[0]):
            for row in range(0, rows, 8):
                value = other[utt, row : row + 8, :]
                for tap in range(8):
                    at = row + first + tap + 1
                    running[tap] = running[tap] + padded[utt, at : at + 8, :] * value
        for tap in range(8):
            store(first + tap, jnp.sum(running[tap], axis=0, keepdims=True))


def early_kernel(place, before, own, convolved, stats, early, padded, centred):
    utts, rows = own.shape[0], own.shape[1]
    mean = stats[0, 0:1, :] / jnp.maximum(stats[0, 2:3, :], 1.0)
    fill_padded(place, padded, before, own, None)
    ones = jnp.zeros((HALO, LANES), f32)
    for utt in range(utts):
        limit = limit_of(place, utt, utts, rows)
        centred[utt] = masked_rows(convolved[utt] - mean, 0, limit)
        lag = (
            lax.broadcasted_iota(jnp.int32, (HALO, HALO + rows), 1)
            - lax.broadcasted_iota(jnp.int32, (HALO, HALO + rows), 0)
            - 1
        )
        band = jnp.where((lag >= 0) & (lag < jnp.minimum(limit, rows)), 1.0, 0.0).astype(bf16)
        ones = ones + jnp.dot(band, padded[utt].astype(bf16), preferred_element_type=f32)
    early[0:32, :] = ones

    def store(tap, value):
        early[32 + tap : 33 + tap, :] = value

    correlate(padded, centred, rows, store)


def early_sums(place, before, own, convolved, stats):
    utts, rows, channels = own.shape
    by_tile = lambda j, s: (0, 0, j)
    return pl.pallas_call(
        early_kernel,
        grid_spec=pltpu.PrefetchScalarGridSpec(
            num_scalar_prefetch=1,
            grid=(channels // LANES,),
            in_specs=[
                pl.BlockSpec((utts, HALO, LANES), by_tile),
                pl.BlockSpec((utts, rows, LANES), by_tile),
                pl.BlockSpec((utts, rows, LANES), by_tile),
                pl.BlockSpec((1, 3, LANES), stats_place(channels // 4 // LANES)),
            ],
            out_specs=pl.BlockSpec((64, LANES), lambda j, s: (0, j)),
            scratch_shapes=[
                pltpu.VMEM((utts, HALO + rows, LANES), f32),
                pltpu.VMEM((utts, rows, LANES), f32),
            ],
        ),
        out_shape=jax.ShapeDtypeStruct((64, channels), f32),
        compiler_params=pltpu.CompilerParams(vmem_limit_bytes=24 << 20),
        cost_estimate=pl.CostEstimate(flops=30_000_000, bytes_accessed=4_000_000, transcendentals=0),
    )(place, before, own, convolved, stats)


def late_kernel(
    place, params, before, own, convolved, act_grad, stats, early, sums, pre_out, normed_out, ends_out, padded, pre
):
    utts, rows = own.shape[0], own.shape[1]
    mean, inverse, gain, shift = (params[i : i + 1, :] for i in range(4))
    bias_sum = jnp.zeros((1, LANES), f32)
    gain_sum = jnp.zeros((1, LANES), f32)
    fill_padded(place, padded, before, own, None)
    for utt in range(utts):
        limit = limit_of(place, utt, utts, rows)
        for start in range(0, rows, 32):
            normed = (convolved[utt, start : start + 32, :] - mean) * inverse
            preact = normed * gain + shift
            sigmoid = jax.nn.sigmoid(preact)
            grad = act_grad[utt, start : start + 32, :] * sigmoid * (1.0 + preact * (1.0 - sigmoid))
            grad = masked_rows(grad, start, limit)
            normed = masked_rows(normed, start, limit)
            pre_out[utt, start : start + 32, :] = grad
            normed_out[utt, start : start + 32, :] = normed
            pre[utt, start : start + 32, :] = grad
            bias_sum = bias_sum + jnp.sum(grad, axis=0, keepdims=True)
            gain_sum = gain_sum + jnp.sum(grad * normed, axis=0, keepdims=True)
            if start == 0:
                ends_out[utt] = grad.astype(bf16)
                ends_out[utts + utt] = normed.astype(bf16)
    column = pl.program_id(0) // (pl.num_programs(0) // 4) >> 1
    near = (column - chip_of(place) & 3) >> 1

    def store(tap, value):
        sums[0, 0, near, tap : tap + 1, :] = value

    correlate(padded, pre, rows, store)
    ones = early[0:32, :]
    own_mean = stats[0, 0:1, :] / jnp.maximum(stats[0, 2:3, :], 1.0)
    sums[0, 0, near, 32:64, :] = ones
    sums[0, 0, near, 64:72, :] = jnp.zeros((8, LANES), f32) + bias_sum
    sums[0, 0, 1 - near, 0:32, :] = (early[32:64, :] + (own_mean - mean) * ones) * inverse
    sums[0, 0, 1 - near, 32:64, :] = jnp.zeros((32, LANES), f32)
    sums[0, 0, 1 - near, 64:72, :] = jnp.zeros((8, LANES), f32) + gain_sum


def late_sums(place, params, before, own, convolved, act_grad, stats, early):
    utts, rows, channels = own.shape
    block_tiles = channels // 4 // LANES

    def slot(j, s):
        column = j // block_tiles
        return ((column ^ s[9]) & 1, ((column >> 1) ^ (s[9] >> 1)) & 1, 0, 0, j % block_tiles)

    by_tile = lambda j, s: (0, 0, j)
    by_column = lambda j, s: (0, j)
    return pl.pallas_call(
        late_kernel,
        grid_spec=pltpu.PrefetchScalarGridSpec(
            num_scalar_prefetch=1,
            grid=(channels // LANES,),
            in_specs=[
                pl.BlockSpec((4, LANES), by_column),
                pl.BlockSpec((utts, HALO, LANES), by_tile),
                pl.BlockSpec((utts, rows, LANES), by_tile),
                pl.BlockSpec((utts, rows, LANES), by_tile),
                pl.BlockSpec((utts, rows, LANES), by_tile),
                pl.BlockSpec((1, 3, LANES), stats_place(block_tiles)),
                pl.BlockSpec((64, LANES), by_column),
            ],
            out_specs=[
                pl.BlockSpec((1, 1, 2, 72, LANES), slot),
                pl.BlockSpec((utts, rows, LANES), by_tile),
                pl.BlockSpec((utts, rows, LANES), by_tile),
                pl.BlockSpec((2 * utts, HALO, LANES), by_tile),
            ],
            scratch_shapes=[
                pltpu.VMEM((utts, HALO + rows, LANES), f32),
                pltpu.VMEM((utts, rows, LANES), f32),
            ],
        ),
        out_shape=[
            jax.ShapeDtypeStruct((2, 2, 2, 72, channels // 4), f32),
            jax.ShapeDtypeStruct((utts, rows, channels), f32),
            jax.ShapeDtypeStruct((utts, rows, channels), f32),
            jax.ShapeDtypeStruct((2 * utts, HALO, channels), bf16),
        ],
        compiler_params=pltpu.CompilerParams(vmem_limit_bytes=24 << 20),
        cost_estimate=pl.CostEstimate(flops=40_000_000, bytes_accessed=10_000_000, transcendentals=500_000),
    )(place, params, before, own, convolved, act_grad, stats, early)


def back_kernel(place, taps, params, pre, normed, ahead, out, grad):
    utts, rows = out.shape[0], out.shape[1]
    scale, bias_mean, gain_mean = (params[i : i + 1, :] for i in range(3))
    for utt in range(utts):
        limit = limit_of(place, utt, utts, rows)
        value = pre[utt] - bias_mean - normed[utt] * gain_mean
        grad[utt, 0:rows, :] = masked_rows(value * scale, 0, limit)
        value = ahead[utt].astype(f32) - bias_mean - ahead[utts + utt].astype(f32) * gain_mean
        grad[utt, rows:, :] = masked_rows(value * scale, rows, limit)
        for start in range(0, rows, 64):
            result = jnp.zeros((64, LANES), f32)
            for lead in range(HALO):
                tap = HALO - 1 - lead
                result = result + taps[tap : tap + 1, :] * grad[utt, start + lead : start + lead + 64, :]
            out[utt, start : start + 64, :] = masked_rows(result, start, limit).astype(bf16)


def frames_back(place, taps, params, pre, normed, ahead):
    utts, rows, channels = pre.shape
    by_tile = lambda j, s: (0, 0, j)
    return pl.pallas_call(
        back_kernel,
        grid_spec=pltpu.PrefetchScalarGridSpec(
            num_scalar_prefetch=1,
            grid=(channels // LANES,),
            in_specs=[
                pl.BlockSpec((HALO, LANES), lambda j, s: (0, j)),
                pl.BlockSpec((3, LANES), lambda j, s: (0, j)),
                pl.BlockSpec((utts, rows, LANES), by_tile),
                pl.BlockSpec((utts, rows, LANES), by_tile),
                pl.BlockSpec((2 * utts, HALO, LANES), by_tile),
            ],
            out_specs=pl.BlockSpec((utts, rows, LANES), by_tile),
            scratch_shapes=[pltpu.VMEM((utts, rows + HALO, LANES), f32)],
        ),
        out_shape=jax.ShapeDtypeStruct((utts, rows, channels), bf16),
        compiler_params=pltpu.CompilerParams(vmem_limit_bytes=24 << 20),
        cost_estimate=pl.CostEstimate(flops=30_000_000, bytes_accessed=5_000_000, transcendentals=0),
    )(place, taps, params, pre, normed, ahead)


def widen_kernel(place, value, *refs):
    refs[-1][0] = value[...].astype(f32)


def widened(place, value, other, whole):
    half, block = value.shape
    aliased = whole is not None
    return pl.pallas_call(
        widen_kernel,
        grid_spec=pltpu.PrefetchScalarGridSpec(
            num_scalar_prefetch=1,
            grid=(2,),
            in_specs=[pl.BlockSpec((half // 2, block), lambda i, s: (i, 0))]
            + [pl.BlockSpec(memory_space=pl.ANY)] * aliased,
            out_specs=pl.BlockSpec((1, half // 2, block), lambda i, s: ((s[8] & 1) ^ other, i, 0)),
        ),
        out_shape=jax.ShapeDtypeStruct((2, half, block), f32),
        input_output_aliases={2: 0} if aliased else {},
        compiler_params=pltpu.CompilerParams(vmem_limit_bytes=16 << 20),
        cost_estimate=pl.CostEstimate(flops=half * block, bytes_accessed=6 * half * block, transcendentals=0),
    )(place, value, *([whole] if aliased else []))


def moved(value, steps):
    count = lax.axis_size("tm")
    return lax.ppermute(value, "tm", [(i, i + steps) for i in range(count) if 0 <= i + steps < count])


def other_core(value):
    return lax.ppermute(value, "fsdp", [(0, 1), (1, 0), (2, 3), (3, 2)])


def other_chip(value):
    return lax.ppermute(value, "fsdp", [(0, 2), (2, 0), (1, 3), (3, 1)])


def across(value):
    return lax.ppermute(value, "tm", [(i, i ^ 1) for i in range(lax.axis_size("tm"))])


def along(value, steps):
    pairs = []
    for device in range(4 * lax.axis_size("tm")):
        plane, high, low, core = device // 8, device // 4 % 2, device // 2 % 2, device % 2
        place = (high * 2 + low + steps) % 4
        pairs.append((device, plane * 8 + place // 2 * 4 + place % 2 * 2 + core))
    return lax.ppermute(value, ("tm", "fsdp"), pairs)


def in_plane(value):
    count = lax.axis_size("tm")
    groups = [list(range(start, count, 2)) for start in range(2)]
    return lax.all_to_all(value, "tm", 0, 0, axis_index_groups=groups, tiled=True)


def from_all(value, chip, core):
    by_core = other_core(value)
    pair = jnp.where(core == 0, jnp.stack([value, by_core]), jnp.stack([by_core, value]))
    by_chip = other_chip(pair)
    return jnp.where(chip == 0, jnp.concatenate([pair, by_chip]), jnp.concatenate([by_chip, pair]))


def in_three(value):
    first = lax.reduce_precision(value, 8, 7)
    second = lax.reduce_precision(value - first, 8, 7)
    third = value - first - second
    return first.astype(bf16), second.astype(bf16), third.astype(bf16)


def on_device(frames_in, lengths, depth_kernel, norm_gain, norm_bias, out_weight, cotangent):
    utts, rows, channels = frames_in.shape
    tm, fsdp = lax.axis_index("tm"), lax.axis_index("fsdp")
    tm_count, fsdp_count = lax.axis_size("tm"), lax.axis_size("fsdp")
    block, half = channels // fsdp_count, channels // 2
    chip, core, high = fsdp // 2, fsdp % 2, tm % 2
    frames_valid = jnp.sum(lengths).astype(f32)
    table = [side for side, _ in QUARTERS] + [row for _, row in QUARTERS]
    scalars = jnp.concatenate(
        [lengths, jnp.stack([tm, fsdp]).astype(jnp.int32), jnp.array(table, jnp.int32)]
    )

    whole_weight = lax.all_gather(out_weight, "fsdp", axis=1, tiled=True)
    before = moved(frames_in[:, rows - HALO :, :], 1)
    convolved, stats = depthwise(scalars, depth_kernel, before, frames_in)

    plane = tm_count // 2
    chip_stats = in_vmem(pair_kernel, (3, half), stats, other_core(stats[1]))
    pieces = in_vmem(
        ring_kernel,
        (plane, 16, LANES),
        chip_stats,
        along(chip_stats, 1),
        along(chip_stats, -1),
        along(chip_stats, 2),
    )
    pieces, early_frames = lax.optimization_barrier((pieces, frames_in))
    pieces = in_plane(pieces)
    early = early_sums(scalars, before, early_frames, convolved, stats)
    pieces, early = lax.optimization_barrier((pieces, early))
    mine = in_vmem(moments_kernel, (2, half), lengths, pieces, scalars=1)
    params = in_vmem(
        params_kernel,
        (4, channels),
        scalars,
        mine,
        other_core(mine),
        norm_gain[None],
        norm_bias[None],
        scalars=1,
    )

    active, send_first, send_rest, keep_first, keep_rest = weight_terms(scalars, convolved, params, cotangent)
    got_first, got_rest = other_core(send_first), other_core(send_rest)
    upward = (keep_first[:2] + got_first[:2].astype(f32)).astype(bf16)
    downward = (keep_first[2:] + got_first[2:].astype(f32)).astype(bf16)
    upward, downward, out_grads = lax.optimization_barrier((upward, downward, cotangent))
    below, above = along(upward, 1), along(downward, -1)
    act_grad = lax.dot_general(
        out_grads.reshape(utts * rows, channels),
        whole_weight,
        (((1,), (1,)), ((), ())),
        preferred_element_type=f32,
    ).reshape(frames_in.shape)
    sums, pre, normed, first_rows = late_sums(
        scalars, params, before, frames_in, convolved, act_grad, stats, early
    )
    near_sums = sums[0] + other_core(sums[1])

    rest = keep_rest + got_rest.astype(f32)
    upward = (rest[0] + below[0].astype(f32)).astype(bf16)
    downward = (rest[1] + above[0].astype(f32)).astype(bf16)
    upward, downward, near_sums, first_rows = lax.optimization_barrier(
        (upward, downward, near_sums, first_rows)
    )
    base = jnp.concatenate([rest[2] + above[1].astype(f32), rest[3] + below[1].astype(f32)], 0)
    below, above = along(upward, 1), along(downward, -1)
    kept = (
        near_sums[0, 0]
        + along(near_sums[1, 0], 1)
        + along(near_sums[0, 1], 2)
        + along(near_sums[1, 1], -1)
    )

    outgoing = packed(base, below, above, kept, plane)
    incoming = in_plane(outgoing)
    summed = jnp.sum(incoming.astype(f32), axis=0)
    weight_rows = half // plane
    ride = summed[weight_rows : weight_rows + 3] + summed[weight_rows + 3 : weight_rows + 6]
    piece = summed[:weight_rows].astype(bf16)
    piece, ride, first_rows = lax.optimization_barrier((piece, ride, first_rows))
    ahead = moved(first_rows, -1)
    gathered = in_plane(jnp.broadcast_to(piece, (plane, *piece.shape)))

    far_ride = across(ride)
    by_high = jnp.where(high == 0, jnp.stack([ride, far_ride]), jnp.stack([far_ride, ride]))
    ends = by_high[:, 2] / frames_valid
    gain_scale = lax.dynamic_slice_in_dim(norm_gain * params[1], fsdp * block, block, 0)
    kernel_own = gain_scale * (by_high[0, 0] - ends[0] * by_high[0, 1] - ends[1] * by_high[1, 0])
    rows_own = jnp.concatenate([by_high[:, 2], kernel_own[None]], 0)
    whole_rows = from_all(rows_own, chip, core).transpose(1, 0, 2).reshape(3, channels)
    bias_grad, gain_grad = whole_rows[0], whole_rows[1]
    back_params = jnp.concatenate([(norm_gain * params[1])[None], whole_rows[:2] / frames_valid], 0)
    frames_grad = frames_back(scalars, depth_kernel, back_params, pre, normed, ahead)

    mine = gathered.reshape(half, block)
    mine, active, kernel_row = lax.optimization_barrier((mine, active, whole_rows[2:]))
    theirs = across(mine)
    kernel_row = kernel_row.reshape(channels // LANES, LANES)
    kernel_row = jnp.concatenate([kernel_row, kernel_row[: 16 - channels // LANES]], 0)
    kernel_rows = in_plane(jnp.broadcast_to(kernel_row, (plane, 16, LANES)))
    kernel_grad = kernel_rows[:, : channels // LANES].reshape(plane, channels)
    mixed = jnp.dot(active, whole_weight, preferred_element_type=f32).astype(bf16).reshape(frames_in.shape)
    weight_grad = widened(scalars, theirs, 1, widened(scalars, mine, 0, None)).reshape(channels, block)
    return (mixed, frames_grad, weight_grad, kernel_grad, gain_grad, bias_grad)


def solution(mesh):
    in_specs = (P("fsdp", "tm", None), P(), P(), P(), P(), P(None, "fsdp"), P("fsdp", "tm", None))
    out_specs = (P("fsdp", "tm", None), P("fsdp", "tm", None), P(None, "fsdp"), P(), P(), P())
    return jax.shard_map(
        on_device, mesh=mesh, in_specs=in_specs, out_specs=out_specs, check_vma=False
    )
```

```python
import functools
import jax
import jax.numpy as jnp
from jax import lax
from jax.experimental import pallas as pl
from jax.experimental.pallas import tpu as pltpu
from jax.sharding import PartitionSpec as P

epsilon = 1e-05
LANES = 128
HALO = 32
f32, bf16 = jnp.float32, jnp.bfloat16


def masked_rows(value, first, limit):
    rows = first + lax.broadcasted_iota(jnp.int32, value.shape, 0)
    return jnp.where(rows < limit, value.astype(f32), 0.0)


def limit_of(place, utt, utts, rows):
    return place[place[9] * utts + utt] - place[8] * rows


def chip_of(place):
    return (place[8] & 1) * 2 + (place[9] >> 1)


def conv_kernel(place, taps, before, own, convolved, stats, padded):
    utts, rows = own.shape[0], own.shape[1]
    total = jnp.zeros((1, LANES), f32)
    valid_count = 0.0
    for utt in range(utts):
        limit = limit_of(place, utt, utts, rows)
        padded[utt, 0:HALO, :] = masked_rows(before[utt], -HALO, limit)
        padded[utt, HALO : HALO + rows, :] = masked_rows(own[utt], 0, limit)
        for start in range(0, rows, 64):
            result = jnp.zeros((64, LANES), f32)
            for tap in range(HALO):
                result = result + taps[tap : tap + 1, :] * padded[utt, start + tap + 1 : start + tap + 65, :]
            convolved[utt, start : start + 64, :] = result
            total = total + jnp.sum(masked_rows(result, start, limit), axis=0, keepdims=True)
        valid_count = valid_count + jnp.clip(limit, 0, rows).astype(f32)
    mean = total / jnp.maximum(valid_count, 1.0)
    squares = jnp.zeros((1, LANES), f32)
    for utt in range(utts):
        centred = masked_rows(convolved[utt] - mean, 0, limit_of(place, utt, utts, rows))
        squares = squares + jnp.sum(centred * centred, axis=0, keepdims=True)
    stats[0, 0:1, :] = total
    stats[0, 1:2, :] = squares
    stats[0, 2:3, :] = jnp.zeros((1, LANES), f32) + valid_count


def stats_place(tiles):
    def index(j, s):
        column = j // tiles
        return ((column ^ s[9]) & 1, 0, (column >> 1) * tiles + j % tiles)

    return index


def merge_rows(parts):
    count = sum(part[2:3, :] for part in parts)
    total = sum(part[0:1, :] for part in parts)
    mean = total / jnp.maximum(count, 1.0)
    squares = jnp.zeros_like(mean)
    for part in parts:
        apart = part[0:1, :] / jnp.maximum(part[2:3, :], 1.0) - mean
        squares = squares + part[1:2, :] + part[2:3, :] * apart * apart
    return total, squares, count


def pair_kernel(own, got, out):
    total, squares, count = merge_rows([own[0], got[...]])
    out[0:1, :] = total
    out[1:2, :] = squares
    out[2:3, :] = count


def ring_kernel(own, first, second, third, out):
    total, squares, count = merge_rows([own[...], first[...], second[...], third[...]])
    tiles = total.shape[1] // LANES
    rows = [value[:, i * LANES : (i + 1) * LANES] for value in (total, squares) for i in range(tiles)]
    rows += [count[:, 0:LANES]] * (out.shape[1] - 2 * tiles)
    out[...] = jnp.broadcast_to(jnp.concatenate(rows, 0)[None], out.shape)


def moments_kernel(lengths, pieces, out):
    tiles = out.shape[1] // LANES
    total, squares = pieces[:, 0:tiles, :], pieces[:, tiles : 2 * tiles, :]
    counts = pieces[:, 2 * tiles : 2 * tiles + 1, :]
    valid = lengths[0]
    for utt in range(1, lengths.shape[0]):
        valid = valid + lengths[utt]
    mean = jnp.sum(total, axis=0) / jnp.sum(counts, axis=0)
    apart = total / jnp.maximum(counts, 1.0) - mean[None]
    variance = jnp.sum(squares + counts * apart * apart, axis=0) / (jnp.zeros_like(mean) + valid.astype(f32))
    inverse = lax.rsqrt(variance + epsilon)
    for i in range(tiles):
        out[0:1, i * LANES : (i + 1) * LANES] = mean[i : i + 1, :]
        out[1:2, i * LANES : (i + 1) * LANES] = inverse[i : i + 1, :]


def params_kernel(place, mine, theirs, gain, shift, out):
    block = gain.shape[1] // 4
    core = place[9] & 1
    for chip in range(2):
        part = slice(chip * block, (chip + 1) * block)
        first = pl.multiple_of(chip * 2 * block + core * block, LANES)
        second = pl.multiple_of(chip * 2 * block + (1 - core) * block, LANES)
        out[0:2, pl.ds(first, block)] = mine[:, part]
        out[0:2, pl.ds(second, block)] = theirs[:, part]
    out[2:3, :] = gain[...]
    out[3:4, :] = shift[...]


def in_vmem(kernel, shape, *operands, scalars=0):
    smem, vmem = pl.BlockSpec(memory_space=pltpu.SMEM), pl.BlockSpec(memory_space=pltpu.VMEM)
    return pl.pallas_call(
        kernel,
        in_specs=[smem] * scalars + [vmem] * (len(operands) - scalars),
        out_specs=vmem,
        out_shape=jax.ShapeDtypeStruct(shape, f32),
        compiler_params=pltpu.CompilerParams(vmem_limit_bytes=16 << 20),
        cost_estimate=pl.CostEstimate(flops=100_000, bytes_accessed=50_000, transcendentals=0),
    )(*operands)


def depthwise(place, taps, before, own):
    utts, rows, channels = own.shape
    tiles = channels // LANES
    return pl.pallas_call(
        conv_kernel,
        grid_spec=pltpu.PrefetchScalarGridSpec(
            num_scalar_prefetch=1,
            grid=(tiles,),
            in_specs=[
                pl.BlockSpec((HALO, LANES), lambda j, s: (0, j)),
                pl.BlockSpec((utts, HALO, LANES), lambda j, s: (0, 0, j)),
                pl.BlockSpec((utts, rows, LANES), lambda j, s: (0, 0, j)),
            ],
            out_specs=[
                pl.BlockSpec((utts, rows, LANES), lambda j, s: (0, 0, j)),
                pl.BlockSpec((1, 3, LANES), stats_place(tiles // 4)),
            ],
            scratch_shapes=[pltpu.VMEM((utts, HALO + rows, LANES), f32)],
        ),
        out_shape=[
            jax.ShapeDtypeStruct(own.shape, f32),
            jax.ShapeDtypeStruct((2, 3, channels // 2), f32),
        ],
        compiler_params=pltpu.CompilerParams(vmem_limit_bytes=24 << 20),
        cost_estimate=pl.CostEstimate(flops=30_000_000, bytes_accessed=3_000_000, transcendentals=0),
    )(place, taps, before, own)


QUARTERS = ((2, 0), (1, 1), (2, 1), (3, 0), (1, 0), (3, 1), (0, 0), (0, 1))


def quarter_term(place, active, grads, quarter):
    size = active.shape[1] // 4
    side, row = place[10 + quarter], place[18 + quarter]
    first = pl.multiple_of(((chip_of(place) + side & 3) >> 1) * (2 * size) + row * size, LANES)
    masked = jnp.concatenate([grads[utt] for utt in range(grads.shape[0])], 0)
    return lax.dot_general(
        active[:, pl.ds(first, size)], masked, (((0,), (0,)), ((), ())), preferred_element_type=f32
    )


def send_kernel(place, convolved, params, grads_even, grads_odd, active_out, first, rest, active):
    utts, rows, channels = convolved.shape
    step = pl.program_id(0)

    @pl.when(step == 0)
    def _():
        for utt in range(utts):
            limit = limit_of(place, utt, utts, rows)
            for start in range(0, rows, 32):
                normed = (convolved[utt, start : start + 32, :] - params[0:1, :]) * params[1:2, :]
                preact = normed * params[2:3, :] + params[3:4, :]
                value = masked_rows(jax.nn.silu(preact), start, limit).astype(bf16)
                at = utt * rows + start
                active[at : at + 32, :] = value
                active_out[at : at + 32, :] = value

    even = quarter_term(place, active, grads_even, 2 * step).astype(bf16)
    odd = quarter_term(place, active, grads_odd, 2 * step + 1).astype(bf16)

    @pl.when(step < 2)
    def _():
        first[0] = even
        first[1] = odd

    @pl.when(step >= 2)
    def _():
        rest[0] = even
        rest[1] = odd


def keep_kernel(place, active, grads_even, grads_odd, first, rest):
    step = pl.program_id(0)
    even = quarter_term(place, active, grads_even, 2 * step)
    odd = quarter_term(place, active, grads_odd, 2 * step + 1)

    @pl.when(step < 2)
    def _():
        first[0] = even
        first[1] = odd

    @pl.when(step >= 2)
    def _():
        rest[0] = even
        rest[1] = odd


def weight_terms(place, convolved, params, reach_grad):
    utts, rows, channels = convolved.shape
    block = channels // 4
    whole = utts * rows

    def column(odd, other):
        return lambda i, s: (
            0,
            0,
            (chip_of(s) + s[10 + 2 * i + odd] & 1) * 2 + ((s[9] & 1) ^ other),
        )

    early = lambda i, s: (jnp.minimum(i, 1), 0, 0)
    late = lambda i, s: (jnp.maximum(i - 2, 0), 0, 0)
    active, send_first, send_rest = pl.pallas_call(
        send_kernel,
        grid_spec=pltpu.PrefetchScalarGridSpec(
            num_scalar_prefetch=1,
            grid=(4,),
            in_specs=[
                pl.BlockSpec((utts, rows, channels), lambda i, s: (0, 0, 0)),
                pl.BlockSpec((4, channels), lambda i, s: (0, 0)),
                pl.BlockSpec((utts, rows, block), column(0, 1)),
                pl.BlockSpec((utts, rows, block), column(1, 1)),
            ],
            out_specs=[
                pl.BlockSpec((whole, channels), lambda i, s: (0, 0)),
                pl.BlockSpec((2, block, block), early),
                pl.BlockSpec((2, block, block), late),
            ],
            scratch_shapes=[pltpu.VMEM((whole, channels), bf16)],
        ),
        out_shape=[
            jax.ShapeDtypeStruct((whole, channels), bf16),
            jax.ShapeDtypeStruct((4, block, block), bf16),
            jax.ShapeDtypeStruct((4, block, block), bf16),
        ],
        compiler_params=pltpu.CompilerParams(vmem_limit_bytes=24 << 20),
        cost_estimate=pl.CostEstimate(
            flops=whole * channels * channels, bytes_accessed=6_000_000, transcendentals=whole * channels
        ),
    )(place, convolved, params, reach_grad, reach_grad)
    keep_first, keep_rest = pl.pallas_call(
        keep_kernel,
        grid_spec=pltpu.PrefetchScalarGridSpec(
            num_scalar_prefetch=1,
            grid=(4,),
            in_specs=[
                pl.BlockSpec((whole, channels), lambda i, s: (0, 0)),
                pl.BlockSpec((utts, rows, block), column(0, 0)),
                pl.BlockSpec((utts, rows, block), column(1, 0)),
            ],
            out_specs=[
                pl.BlockSpec((2, block, block), early),
                pl.BlockSpec((2, block, block), late),
            ],
        ),
        out_shape=[jax.ShapeDtypeStruct((4, block, block), f32)] * 2,
        compiler_params=pltpu.CompilerParams(vmem_limit_bytes=24 << 20),
        cost_estimate=pl.CostEstimate(
            flops=whole * channels * channels, bytes_accessed=6_000_000, transcendentals=0
        ),
    )(place, active, reach_grad, reach_grad)
    return active, send_first, send_rest, keep_first, keep_rest


def pack_kernel(base, low, high, sums, out):
    groups, size = out.shape[0], out.shape[1] - 8
    first = pl.program_id(0) * groups
    total = base[...] + jnp.where(pl.program_id(0) < 2, low[...].astype(f32), high[...].astype(f32))
    filler = jnp.zeros((2, total.shape[1]), f32)
    for group in range(groups):
        row = first + group
        ride = jnp.concatenate([sums[pl.ds(row, 1), :], sums[pl.ds(32 + row, 1), :], sums[64:65, :]], 0)
        rounded = ride.astype(bf16).astype(f32)
        out[group] = jnp.concatenate(
            [total[group * size : (group + 1) * size], rounded, ride - rounded, filler], 0
        ).astype(bf16)


def packed(base, low, high, sums, count):
    half, block = base.shape
    size = half // count
    groups = count // 4
    by_rows = lambda i: (i, 0)
    return pl.pallas_call(
        pack_kernel,
        grid=(count // groups,),
        in_specs=[
            pl.BlockSpec((groups * size, block), by_rows),
            pl.BlockSpec((groups * size, block), lambda i: (jnp.minimum(i, 1), 0)),
            pl.BlockSpec((groups * size, block), lambda i: (jnp.maximum(i - 2, 0), 0)),
            pl.BlockSpec(sums.shape, lambda i: (0, 0)),
        ],
        out_specs=pl.BlockSpec((groups, size + 8, block), lambda i: (i, 0, 0)),
        out_shape=jax.ShapeDtypeStruct((count, size + 8, block), bf16),
        compiler_params=pltpu.CompilerParams(vmem_limit_bytes=16 << 20),
        cost_estimate=pl.CostEstimate(flops=2_000_000, bytes_accessed=4_000_000, transcendentals=0),
    )(base, low, high, sums)


def fill_padded(place, padded, before, own, after):
    utts, rows = own.shape[0], own.shape[1]
    for utt in range(utts):
        limit = limit_of(place, utt, utts, rows)
        padded[utt, 0:HALO, :] = masked_rows(before[utt], -HALO, limit)
        padded[utt, HALO : HALO + rows, :] = masked_rows(own[utt], 0, limit)
        if after is not None:
            padded[utt, HALO + rows :, :] = masked_rows(after[utt], rows, limit)


def correlate(padded, other, rows, store):
    for first in range(0, HALO, 8):
        running = [jnp.zeros((8, LANES), f32) for _ in range(8)]
        for utt in range(padded.shape[0]):
            for row in range(0, rows, 8):
                value = other[utt, row : row + 8, :]
                for tap in range(8):
                    at = row + first + tap + 1
                    running[tap] = running[tap] + padded[utt, at : at + 8, :] * value
        for tap in range(8):
            store(first + tap, jnp.sum(running[tap], axis=0, keepdims=True))


def early_kernel(place, before, own, convolved, stats, early, padded, centred):
    utts, rows = own.shape[0], own.shape[1]
    mean = stats[0, 0:1, :] / jnp.maximum(stats[0, 2:3, :], 1.0)
    fill_padded(place, padded, before, own, None)
    ones = jnp.zeros((HALO, LANES), f32)
    for utt in range(utts):
        limit = limit_of(place, utt, utts, rows)
        centred[utt] = masked_rows(convolved[utt] - mean, 0, limit)
        lag = (
            lax.broadcasted_iota(jnp.int32, (HALO, HALO + rows), 1)
            - lax.broadcasted_iota(jnp.int32, (HALO, HALO + rows), 0)
            - 1
        )
        band = jnp.where((lag >= 0) & (lag < jnp.minimum(limit, rows)), 1.0, 0.0).astype(bf16)
        ones = ones + jnp.dot(band, padded[utt].astype(bf16), preferred_element_type=f32)
    early[0:32, :] = ones

    def store(tap, value):
        early[32 + tap : 33 + tap, :] = value

    correlate(padded, centred, rows, store)


def early_sums(place, before, own, convolved, stats):
    utts, rows, channels = own.shape
    by_tile = lambda j, s: (0, 0, j)
    return pl.pallas_call(
        early_kernel,
        grid_spec=pltpu.PrefetchScalarGridSpec(
            num_scalar_prefetch=1,
            grid=(channels // LANES,),
            in_specs=[
                pl.BlockSpec((utts, HALO, LANES), by_tile),
                pl.BlockSpec((utts, rows, LANES), by_tile),
                pl.BlockSpec((utts, rows, LANES), by_tile),
                pl.BlockSpec((1, 3, LANES), stats_place(channels // 4 // LANES)),
            ],
            out_specs=pl.BlockSpec((64, LANES), lambda j, s: (0, j)),
            scratch_shapes=[
                pltpu.VMEM((utts, HALO + rows, LANES), f32),
                pltpu.VMEM((utts, rows, LANES), f32),
            ],
        ),
        out_shape=jax.ShapeDtypeStruct((64, channels), f32),
        compiler_params=pltpu.CompilerParams(vmem_limit_bytes=24 << 20),
        cost_estimate=pl.CostEstimate(flops=30_000_000, bytes_accessed=4_000_000, transcendentals=0),
    )(place, before, own, convolved, stats)


def late_kernel(
    place, params, before, own, convolved, act_grad, stats, early, sums, pre_out, normed_out, ends_out, padded, pre
):
    utts, rows = own.shape[0], own.shape[1]
    mean, inverse, gain, shift = (params[i : i + 1, :] for i in range(4))
    bias_sum = jnp.zeros((1, LANES), f32)
    gain_sum = jnp.zeros((1, LANES), f32)
    fill_padded(place, padded, before, own, None)
    for utt in range(utts):
        limit = limit_of(place, utt, utts, rows)
        for start in range(0, rows, 32):
            normed = (convolved[utt, start : start + 32, :] - mean) * inverse
            preact = normed * gain + shift
            sigmoid = jax.nn.sigmoid(preact)
            grad = act_grad[utt, start : start + 32, :] * sigmoid * (1.0 + preact * (1.0 - sigmoid))
            grad = masked_rows(grad, start, limit)
            normed = masked_rows(normed, start, limit)
            pre_out[utt, start : start + 32, :] = grad
            normed_out[utt, start : start + 32, :] = normed
            pre[utt, start : start + 32, :] = grad
            bias_sum = bias_sum + jnp.sum(grad, axis=0, keepdims=True)
            gain_sum = gain_sum + jnp.sum(grad * normed, axis=0, keepdims=True)
            if start == 0:
                ends_out[utt] = grad.astype(bf16)
                ends_out[utts + utt] = normed.astype(bf16)
    column = pl.program_id(0) // (pl.num_programs(0) // 4) >> 1
    near = (column - chip_of(place) & 3) >> 1

    def store(tap, value):
        sums[0, 0, near, tap : tap + 1, :] = value

    correlate(padded, pre, rows, store)
    ones = early[0:32, :]
    own_mean = stats[0, 0:1, :] / jnp.maximum(stats[0, 2:3, :], 1.0)
    sums[0, 0, near, 32:64, :] = ones
    sums[0, 0, near, 64:72, :] = jnp.zeros((8, LANES), f32) + bias_sum
    sums[0, 0, 1 - near, 0:32, :] = (early[32:64, :] + (own_mean - mean) * ones) * inverse
    sums[0, 0, 1 - near, 32:64, :] = jnp.zeros((32, LANES), f32)
    sums[0, 0, 1 - near, 64:72, :] = jnp.zeros((8, LANES), f32) + gain_sum


def late_sums(place, params, before, own, convolved, act_grad, stats, early):
    utts, rows, channels = own.shape
    block_tiles = channels // 4 // LANES

    def slot(j, s):
        column = j // block_tiles
        return ((column ^ s[9]) & 1, ((column >> 1) ^ (s[9] >> 1)) & 1, 0, 0, j % block_tiles)

    by_tile = lambda j, s: (0, 0, j)
    by_column = lambda j, s: (0, j)
    return pl.pallas_call(
        late_kernel,
        grid_spec=pltpu.PrefetchScalarGridSpec(
            num_scalar_prefetch=1,
            grid=(channels // LANES,),
            in_specs=[
                pl.BlockSpec((4, LANES), by_column),
                pl.BlockSpec((utts, HALO, LANES), by_tile),
                pl.BlockSpec((utts, rows, LANES), by_tile),
                pl.BlockSpec((utts, rows, LANES), by_tile),
                pl.BlockSpec((utts, rows, LANES), by_tile),
                pl.BlockSpec((1, 3, LANES), stats_place(block_tiles)),
                pl.BlockSpec((64, LANES), by_column),
            ],
            out_specs=[
                pl.BlockSpec((1, 1, 2, 72, LANES), slot),
                pl.BlockSpec((utts, rows, LANES), by_tile),
                pl.BlockSpec((utts, rows, LANES), by_tile),
                pl.BlockSpec((2 * utts, HALO, LANES), by_tile),
            ],
            scratch_shapes=[
                pltpu.VMEM((utts, HALO + rows, LANES), f32),
                pltpu.VMEM((utts, rows, LANES), f32),
            ],
        ),
        out_shape=[
            jax.ShapeDtypeStruct((2, 2, 2, 72, channels // 4), f32),
            jax.ShapeDtypeStruct((utts, rows, channels), f32),
            jax.ShapeDtypeStruct((utts, rows, channels), f32),
            jax.ShapeDtypeStruct((2 * utts, HALO, channels), bf16),
        ],
        compiler_params=pltpu.CompilerParams(vmem_limit_bytes=24 << 20),
        cost_estimate=pl.CostEstimate(flops=40_000_000, bytes_accessed=10_000_000, transcendentals=500_000),
    )(place, params, before, own, convolved, act_grad, stats, early)


def back_kernel(place, taps, params, pre, normed, ahead, out, grad):
    utts, rows = out.shape[0], out.shape[1]
    scale, bias_mean, gain_mean = (params[i : i + 1, :] for i in range(3))
    for utt in range(utts):
        limit = limit_of(place, utt, utts, rows)
        value = pre[utt] - bias_mean - normed[utt] * gain_mean
        grad[utt, 0:rows, :] = masked_rows(value * scale, 0, limit)
        value = ahead[utt].astype(f32) - bias_mean - ahead[utts + utt].astype(f32) * gain_mean
        grad[utt, rows:, :] = masked_rows(value * scale, rows, limit)
        for start in range(0, rows, 64):
            result = jnp.zeros((64, LANES), f32)
            for lead in range(HALO):
                tap = HALO - 1 - lead
                result = result + taps[tap : tap + 1, :] * grad[utt, start + lead : start + lead + 64, :]
            out[utt, start : start + 64, :] = masked_rows(result, start, limit).astype(bf16)


def frames_back(place, taps, params, pre, normed, ahead):
    utts, rows, channels = pre.shape
    by_tile = lambda j, s: (0, 0, j)
    return pl.pallas_call(
        back_kernel,
        grid_spec=pltpu.PrefetchScalarGridSpec(
            num_scalar_prefetch=1,
            grid=(channels // LANES,),
            in_specs=[
                pl.BlockSpec((HALO, LANES), lambda j, s: (0, j)),
                pl.BlockSpec((3, LANES), lambda j, s: (0, j)),
                pl.BlockSpec((utts, rows, LANES), by_tile),
                pl.BlockSpec((utts, rows, LANES), by_tile),
                pl.BlockSpec((2 * utts, HALO, LANES), by_tile),
            ],
            out_specs=pl.BlockSpec((utts, rows, LANES), by_tile),
            scratch_shapes=[pltpu.VMEM((utts, rows + HALO, LANES), f32)],
        ),
        out_shape=jax.ShapeDtypeStruct((utts, rows, channels), bf16),
        compiler_params=pltpu.CompilerParams(vmem_limit_bytes=24 << 20),
        cost_estimate=pl.CostEstimate(flops=30_000_000, bytes_accessed=5_000_000, transcendentals=0),
    )(place, taps, params, pre, normed, ahead)


def column_starts(place, block):
    chip, core = place[9] >> 1, place[9] & 1
    owners = (chip * 2 + core, (1 - chip) * 2 + core, chip * 2 + 1 - core, (1 - chip) * 2 + 1 - core)
    return [pl.multiple_of(owner * block, LANES) for owner in owners]


def act_kernel(place, grads, *refs):
    weights, out = refs[:-1], refs[-1]
    size, block = weights[1].shape
    utts, rows = grads.shape[0], grads.shape[1]
    columns = [
        jnp.concatenate([grads[utt, :, pl.ds(first, block)] for utt in range(utts)], 0)
        for first in column_starts(place, block)
    ]
    for half in range(2):
        for start in range(0, size, 384):
            part = slice(start, start + 384)
            whole = slice(half * size + start, half * size + start + 384)
            tiles = (weights[0][whole, :], weights[1 + half][part, :], weights[3][whole, :], weights[4 + half][part, :])
            total = jnp.zeros((utts * rows, 384), f32)
            for column, tile in zip(columns, tiles):
                total = total + lax.dot_general(
                    column, tile, (((1,), (1,)), ((), ())), preferred_element_type=f32
                )
            for utt in range(utts):
                out[utt, :, whole] = total[utt * rows : (utt + 1) * rows]


def mixed_kernel(place, active, *refs):
    weights, out = refs[:-1], refs[-1]
    size, block = weights[1].shape
    utts, rows = out.shape[0], out.shape[1]
    first, second = active[:, :size], active[:, size:]
    tiles = (
        (weights[0][:size, :], weights[0][size:, :]),
        (weights[1][...], weights[2][...]),
        (weights[3][:size, :], weights[3][size:, :]),
        (weights[4][...], weights[5][...]),
    )
    for column, (top, bottom) in zip(column_starts(place, block), tiles):
        total = jnp.dot(first, top, preferred_element_type=f32)
        total = total + jnp.dot(second, bottom, preferred_element_type=f32)
        total = total.astype(bf16)
        for utt in range(utts):
            out[utt, :, pl.ds(column, block)] = total[utt * rows : (utt + 1) * rows]


def with_weights(kernel, place, value, weights, shape, dtype):
    smem, vmem = pl.BlockSpec(memory_space=pltpu.SMEM), pl.BlockSpec(memory_space=pltpu.VMEM)
    return pl.pallas_call(
        kernel,
        in_specs=[smem] + [vmem] * (1 + len(weights)),
        out_specs=vmem,
        out_shape=jax.ShapeDtypeStruct(shape, dtype),
        compiler_params=pltpu.CompilerParams(vmem_limit_bytes=28 << 20),
        cost_estimate=pl.CostEstimate(flops=100_000_000, bytes_accessed=2_000_000, transcendentals=0),
    )(place, value, *weights)


def widen_kernel(place, value, *refs):
    refs[-1][0] = value[...].astype(f32)


def widened(place, value, other, whole):
    half, block = value.shape
    aliased = whole is not None
    return pl.pallas_call(
        widen_kernel,
        grid_spec=pltpu.PrefetchScalarGridSpec(
            num_scalar_prefetch=1,
            grid=(2,),
            in_specs=[pl.BlockSpec((half // 2, block), lambda i, s: (i, 0))]
            + [pl.BlockSpec(memory_space=pl.ANY)] * aliased,
            out_specs=pl.BlockSpec((1, half // 2, block), lambda i, s: ((s[8] & 1) ^ other, i, 0)),
        ),
        out_shape=jax.ShapeDtypeStruct((2, half, block), f32),
        input_output_aliases={2: 0} if aliased else {},
        compiler_params=pltpu.CompilerParams(vmem_limit_bytes=16 << 20),
        cost_estimate=pl.CostEstimate(flops=half * block, bytes_accessed=6 * half * block, transcendentals=0),
    )(place, value, *([whole] if aliased else []))


def moved(value, steps):
    count = lax.axis_size("tm")
    return lax.ppermute(value, "tm", [(i, i + steps) for i in range(count) if 0 <= i + steps < count])


def other_core(value):
    return lax.ppermute(value, "fsdp", [(0, 1), (1, 0), (2, 3), (3, 2)])


def other_chip(value):
    return lax.ppermute(value, "fsdp", [(0, 2), (2, 0), (1, 3), (3, 1)])


def across(value):
    return lax.ppermute(value, "tm", [(i, i ^ 1) for i in range(lax.axis_size("tm"))])


def along(value, steps):
    pairs = []
    for device in range(4 * lax.axis_size("tm")):
        plane, high, low, core = device // 8, device // 4 % 2, device // 2 % 2, device % 2
        place = (high * 2 + low + steps) % 4
        pairs.append((device, plane * 8 + place // 2 * 4 + place % 2 * 2 + core))
    return lax.ppermute(value, ("tm", "fsdp"), pairs)


def in_plane(value):
    count = lax.axis_size("tm")
    groups = [list(range(start, count, 2)) for start in range(2)]
    return lax.all_to_all(value, "tm", 0, 0, axis_index_groups=groups, tiled=True)


def from_all(value, chip, core):
    by_core = other_core(value)
    pair = jnp.where(core == 0, jnp.stack([value, by_core]), jnp.stack([by_core, value]))
    by_chip = other_chip(pair)
    return jnp.where(chip == 0, jnp.concatenate([pair, by_chip]), jnp.concatenate([by_chip, pair]))


def in_three(value):
    first = lax.reduce_precision(value, 8, 7)
    second = lax.reduce_precision(value - first, 8, 7)
    third = value - first - second
    return first.astype(bf16), second.astype(bf16), third.astype(bf16)


def on_device(frames_in, lengths, depth_kernel, norm_gain, norm_bias, out_weight, cotangent):
    utts, rows, channels = frames_in.shape
    tm, fsdp = lax.axis_index("tm"), lax.axis_index("fsdp")
    tm_count, fsdp_count = lax.axis_size("tm"), lax.axis_size("fsdp")
    block, half = channels // fsdp_count, channels // 2
    chip, core, high = fsdp // 2, fsdp % 2, tm % 2
    frames_valid = jnp.sum(lengths).astype(f32)
    table = [side for side, _ in QUARTERS] + [row for _, row in QUARTERS]
    scalars = jnp.concatenate(
        [lengths, jnp.stack([tm, fsdp]).astype(jnp.int32), jnp.array(table, jnp.int32)]
    )

    before = moved(frames_in[:, rows - HALO :, :], 1)
    convolved, stats = depthwise(scalars, depth_kernel, before, frames_in)

    plane = tm_count // 2
    chip_stats = in_vmem(pair_kernel, (3, half), stats, other_core(stats[1]))
    pieces = in_vmem(
        ring_kernel,
        (plane, 16, LANES),
        chip_stats,
        along(chip_stats, 1),
        along(chip_stats, -1),
        along(chip_stats, 2),
    )
    pieces, early_frames, columns, core_columns = lax.optimization_barrier(
        (pieces, frames_in, out_weight, other_core(out_weight))
    )
    pieces = in_plane(pieces)
    low_rows = along(columns[:half], 1)
    high_rows = along(columns[half:], -1)
    early = early_sums(scalars, before, early_frames, convolved, stats)
    pieces, early, low_rows, high_rows = lax.optimization_barrier((pieces, early, low_rows, high_rows))
    core_low, core_high = other_core(low_rows), other_core(high_rows)
    mine = in_vmem(moments_kernel, (2, half), lengths, pieces, scalars=1)
    params = in_vmem(
        params_kernel,
        (4, channels),
        scalars,
        mine,
        other_core(mine),
        norm_gain[None],
        norm_bias[None],
        scalars=1,
    )

    active, send_first, send_rest, keep_first, keep_rest = weight_terms(scalars, convolved, params, cotangent)
    send_first, core_low, core_high = lax.optimization_barrier((send_first, core_low, core_high))
    weights = (columns, low_rows, high_rows, core_columns, core_low, core_high)
    got_first, got_rest = other_core(send_first), other_core(send_rest)
    upward = (keep_first[:2] + got_first[:2].astype(f32)).astype(bf16)
    downward = (keep_first[2:] + got_first[2:].astype(f32)).astype(bf16)
    upward, downward, out_grads = lax.optimization_barrier((upward, downward, cotangent))
    below, above = along(upward, 1), along(downward, -1)
    act_grad = with_weights(act_kernel, scalars, out_grads, weights, frames_in.shape, f32)
    sums, pre, normed, first_rows = late_sums(
        scalars, params, before, frames_in, convolved, act_grad, stats, early
    )
    rest = keep_rest + got_rest.astype(f32)
    upward = (rest[0] + below[0].astype(f32)).astype(bf16)
    downward = (rest[1] + above[0].astype(f32)).astype(bf16)
    upward, downward, sums = lax.optimization_barrier((upward, downward, sums))
    near_sums = sums[0] + other_core(sums[1])
    base = jnp.concatenate([rest[2] + above[1].astype(f32), rest[3] + below[1].astype(f32)], 0)
    below, above = along(upward, 1), along(downward, -1)
    kept = (
        near_sums[0, 0]
        + along(near_sums[1, 0], 1)
        + along(near_sums[0, 1], 2)
        + along(near_sums[1, 1], -1)
    )

    outgoing = packed(base, below, above, kept, plane)
    outgoing, active = lax.optimization_barrier((outgoing, active))
    incoming = in_plane(outgoing)
    mixed = with_weights(mixed_kernel, scalars, active, weights, frames_in.shape, bf16)
    incoming, mixed = lax.optimization_barrier((incoming, mixed))
    summed = jnp.sum(incoming.astype(f32), axis=0)
    weight_rows = half // plane
    ride = summed[weight_rows : weight_rows + 3] + summed[weight_rows + 3 : weight_rows + 6]
    piece = summed[:weight_rows].astype(bf16)
    piece, ride, first_rows = lax.optimization_barrier((piece, ride, first_rows))
    ahead = moved(first_rows, -1)
    gathered = in_plane(jnp.broadcast_to(piece, (plane, *piece.shape)))

    far_ride = across(ride)
    by_high = jnp.where(high == 0, jnp.stack([ride, far_ride]), jnp.stack([far_ride, ride]))
    ends = by_high[:, 2] / frames_valid
    gain_scale = lax.dynamic_slice_in_dim(norm_gain * params[1], fsdp * block, block, 0)
    kernel_own = gain_scale * (by_high[0, 0] - ends[0] * by_high[0, 1] - ends[1] * by_high[1, 0])
    rows_own = jnp.concatenate([by_high[:, 2], kernel_own[None]], 0)
    whole_rows = from_all(rows_own, chip, core).transpose(1, 0, 2).reshape(3, channels)
    bias_grad, gain_grad = whole_rows[0], whole_rows[1]
    back_params = jnp.concatenate([(norm_gain * params[1])[None], whole_rows[:2] / frames_valid], 0)
    frames_grad = frames_back(scalars, depth_kernel, back_params, pre, normed, ahead)

    mine = gathered.reshape(half, block)
    mine, kernel_row = lax.optimization_barrier((mine, whole_rows[2:]))
    theirs = across(mine)
    kernel_row = kernel_row.reshape(channels // LANES, LANES)
    kernel_row = jnp.concatenate([kernel_row, kernel_row[: 16 - channels // LANES]], 0)
    kernel_rows = in_plane(jnp.broadcast_to(kernel_row, (plane, 16, LANES)))
    kernel_grad = kernel_rows[:, : channels // LANES].reshape(plane, channels)
    weight_grad = widened(scalars, theirs, 1, widened(scalars, mine, 0, None)).reshape(channels, block)
    return (mixed, frames_grad, weight_grad, kernel_grad, gain_grad, bias_grad)


def solution(mesh):
    in_specs = (P("fsdp", "tm", None), P(), P(), P(), P(), P(None, "fsdp"), P("fsdp", "tm", None))
    out_specs = (P("fsdp", "tm", None), P("fsdp", "tm", None), P(None, "fsdp"), P(), P(), P())
    return jax.shard_map(
        on_device, mesh=mesh, in_specs=in_specs, out_specs=out_specs, check_vma=False
    )
```

```python
import functools
import jax
import jax.numpy as jnp
from jax import lax
from jax.experimental import pallas as pl
from jax.experimental.pallas import tpu as pltpu
from jax.sharding import PartitionSpec as P

epsilon = 1e-05
LANES = 128
HALO = 32
f32, bf16 = jnp.float32, jnp.bfloat16


def masked_rows(value, first, limit):
    rows = first + lax.broadcasted_iota(jnp.int32, value.shape, 0)
    return jnp.where(rows < limit, value.astype(f32), 0.0)


def limit_of(place, utt, utts, rows):
    return place[place[9] * utts + utt] - place[8] * rows


def chip_of(place):
    return (place[8] & 1) * 2 + (place[9] >> 1)


def conv_kernel(place, taps, before, own, convolved, stats, padded):
    utts, rows = own.shape[0], own.shape[1]
    total = jnp.zeros((1, LANES), f32)
    valid_count = 0.0
    for utt in range(utts):
        limit = limit_of(place, utt, utts, rows)
        padded[utt, 0:HALO, :] = masked_rows(before[utt], -HALO, limit)
        padded[utt, HALO : HALO + rows, :] = masked_rows(own[utt], 0, limit)
        for start in range(0, rows, 64):
            result = jnp.zeros((64, LANES), f32)
            for tap in range(HALO):
                result = result + taps[tap : tap + 1, :] * padded[utt, start + tap + 1 : start + tap + 65, :]
            convolved[utt, start : start + 64, :] = result
            total = total + jnp.sum(masked_rows(result, start, limit), axis=0, keepdims=True)
        valid_count = valid_count + jnp.clip(limit, 0, rows).astype(f32)
    mean = total / jnp.maximum(valid_count, 1.0)
    squares = jnp.zeros((1, LANES), f32)
    for utt in range(utts):
        centred = masked_rows(convolved[utt] - mean, 0, limit_of(place, utt, utts, rows))
        squares = squares + jnp.sum(centred * centred, axis=0, keepdims=True)
    stats[0, 0:1, :] = total
    stats[0, 1:2, :] = squares
    stats[0, 2:3, :] = jnp.zeros((1, LANES), f32) + valid_count


def stats_place(tiles):
    def index(j, s):
        column = j // tiles
        return ((column ^ s[9]) & 1, 0, (column >> 1) * tiles + j % tiles)

    return index


def merge_rows(parts):
    count = sum(part[2:3, :] for part in parts)
    total = sum(part[0:1, :] for part in parts)
    mean = total / jnp.maximum(count, 1.0)
    squares = jnp.zeros_like(mean)
    for part in parts:
        apart = part[0:1, :] / jnp.maximum(part[2:3, :], 1.0) - mean
        squares = squares + part[1:2, :] + part[2:3, :] * apart * apart
    return total, squares, count


def pair_kernel(own, got, out):
    total, squares, count = merge_rows([own[0], got[...]])
    out[0:1, :] = total
    out[1:2, :] = squares
    out[2:3, :] = count


def ring_kernel(own, first, second, third, out):
    total, squares, count = merge_rows([own[...], first[...], second[...], third[...]])
    tiles = total.shape[1] // LANES
    rows = [value[:, i * LANES : (i + 1) * LANES] for value in (total, squares) for i in range(tiles)]
    rows += [count[:, 0:LANES]] * (out.shape[1] - 2 * tiles)
    out[...] = jnp.broadcast_to(jnp.concatenate(rows, 0)[None], out.shape)


def moments_kernel(lengths, pieces, out):
    tiles = out.shape[1] // LANES
    total, squares = pieces[:, 0:tiles, :], pieces[:, tiles : 2 * tiles, :]
    counts = pieces[:, 2 * tiles : 2 * tiles + 1, :]
    valid = lengths[0]
    for utt in range(1, lengths.shape[0]):
        valid = valid + lengths[utt]
    mean = jnp.sum(total, axis=0) / jnp.sum(counts, axis=0)
    apart = total / jnp.maximum(counts, 1.0) - mean[None]
    variance = jnp.sum(squares + counts * apart * apart, axis=0) / (jnp.zeros_like(mean) + valid.astype(f32))
    inverse = lax.rsqrt(variance + epsilon)
    for i in range(tiles):
        out[0:1, i * LANES : (i + 1) * LANES] = mean[i : i + 1, :]
        out[1:2, i * LANES : (i + 1) * LANES] = inverse[i : i + 1, :]


def params_kernel(place, mine, theirs, gain, shift, out):
    block = gain.shape[1] // 4
    core = place[9] & 1
    for chip in range(2):
        part = slice(chip * block, (chip + 1) * block)
        first = pl.multiple_of(chip * 2 * block + core * block, LANES)
        second = pl.multiple_of(chip * 2 * block + (1 - core) * block, LANES)
        out[0:2, pl.ds(first, block)] = mine[:, part]
        out[0:2, pl.ds(second, block)] = theirs[:, part]
    out[2:3, :] = gain[...]
    out[3:4, :] = shift[...]


def in_vmem(kernel, shape, *operands, scalars=0):
    smem, vmem = pl.BlockSpec(memory_space=pltpu.SMEM), pl.BlockSpec(memory_space=pltpu.VMEM)
    return pl.pallas_call(
        kernel,
        in_specs=[smem] * scalars + [vmem] * (len(operands) - scalars),
        out_specs=vmem,
        out_shape=jax.ShapeDtypeStruct(shape, f32),
        compiler_params=pltpu.CompilerParams(vmem_limit_bytes=16 << 20),
        cost_estimate=pl.CostEstimate(flops=100_000, bytes_accessed=50_000, transcendentals=0),
    )(*operands)


def depthwise(place, taps, before, own):
    utts, rows, channels = own.shape
    tiles = channels // LANES
    return pl.pallas_call(
        conv_kernel,
        grid_spec=pltpu.PrefetchScalarGridSpec(
            num_scalar_prefetch=1,
            grid=(tiles,),
            in_specs=[
                pl.BlockSpec((HALO, LANES), lambda j, s: (0, j)),
                pl.BlockSpec((utts, HALO, LANES), lambda j, s: (0, 0, j)),
                pl.BlockSpec((utts, rows, LANES), lambda j, s: (0, 0, j)),
            ],
            out_specs=[
                pl.BlockSpec((utts, rows, LANES), lambda j, s: (0, 0, j)),
                pl.BlockSpec((1, 3, LANES), stats_place(tiles // 4)),
            ],
            scratch_shapes=[pltpu.VMEM((utts, HALO + rows, LANES), f32)],
        ),
        out_shape=[
            jax.ShapeDtypeStruct(own.shape, f32),
            jax.ShapeDtypeStruct((2, 3, channels // 2), f32),
        ],
        compiler_params=pltpu.CompilerParams(vmem_limit_bytes=24 << 20),
        cost_estimate=pl.CostEstimate(flops=30_000_000, bytes_accessed=3_000_000, transcendentals=0),
    )(place, taps, before, own)


QUARTERS = ((2, 0), (1, 1), (2, 1), (3, 0), (1, 0), (3, 1), (0, 0), (0, 1))


def quarter_term(place, active, grads, quarter):
    size = active.shape[1] // 4
    side, row = place[10 + quarter], place[18 + quarter]
    first = pl.multiple_of(((chip_of(place) + side & 3) >> 1) * (2 * size) + row * size, LANES)
    masked = jnp.concatenate([grads[utt] for utt in range(grads.shape[0])], 0)
    return lax.dot_general(
        active[:, pl.ds(first, size)], masked, (((0,), (0,)), ((), ())), preferred_element_type=f32
    )


def send_kernel(place, convolved, params, grads_even, grads_odd, active_out, first, rest, active):
    utts, rows, channels = convolved.shape
    step = pl.program_id(0)

    @pl.when(step == 0)
    def _():
        for utt in range(utts):
            limit = limit_of(place, utt, utts, rows)
            for start in range(0, rows, 32):
                normed = (convolved[utt, start : start + 32, :] - params[0:1, :]) * params[1:2, :]
                preact = normed * params[2:3, :] + params[3:4, :]
                value = masked_rows(jax.nn.silu(preact), start, limit).astype(bf16)
                at = utt * rows + start
                active[at : at + 32, :] = value
                active_out[at : at + 32, :] = value

    even = quarter_term(place, active, grads_even, 2 * step).astype(bf16)
    odd = quarter_term(place, active, grads_odd, 2 * step + 1).astype(bf16)

    @pl.when(step < 2)
    def _():
        first[0] = even
        first[1] = odd

    @pl.when(step >= 2)
    def _():
        rest[0] = even
        rest[1] = odd


def keep_kernel(place, active, grads_even, grads_odd, first, rest):
    step = pl.program_id(0)
    even = quarter_term(place, active, grads_even, 2 * step)
    odd = quarter_term(place, active, grads_odd, 2 * step + 1)

    @pl.when(step < 2)
    def _():
        first[0] = even
        first[1] = odd

    @pl.when(step >= 2)
    def _():
        rest[0] = even
        rest[1] = odd


def weight_terms(place, convolved, params, reach_grad):
    utts, rows, channels = convolved.shape
    block = channels // 4
    whole = utts * rows

    def column(odd, other):
        return lambda i, s: (
            0,
            0,
            (chip_of(s) + s[10 + 2 * i + odd] & 1) * 2 + ((s[9] & 1) ^ other),
        )

    early = lambda i, s: (jnp.minimum(i, 1), 0, 0)
    late = lambda i, s: (jnp.maximum(i - 2, 0), 0, 0)
    active, send_first, send_rest = pl.pallas_call(
        send_kernel,
        grid_spec=pltpu.PrefetchScalarGridSpec(
            num_scalar_prefetch=1,
            grid=(4,),
            in_specs=[
                pl.BlockSpec((utts, rows, channels), lambda i, s: (0, 0, 0)),
                pl.BlockSpec((4, channels), lambda i, s: (0, 0)),
                pl.BlockSpec((utts, rows, block), column(0, 1)),
                pl.BlockSpec((utts, rows, block), column(1, 1)),
            ],
            out_specs=[
                pl.BlockSpec((whole, channels), lambda i, s: (0, 0)),
                pl.BlockSpec((2, block, block), early),
                pl.BlockSpec((2, block, block), late),
            ],
            scratch_shapes=[pltpu.VMEM((whole, channels), bf16)],
        ),
        out_shape=[
            jax.ShapeDtypeStruct((whole, channels), bf16),
            jax.ShapeDtypeStruct((4, block, block), bf16),
            jax.ShapeDtypeStruct((4, block, block), bf16),
        ],
        compiler_params=pltpu.CompilerParams(vmem_limit_bytes=24 << 20),
        cost_estimate=pl.CostEstimate(
            flops=whole * channels * channels, bytes_accessed=6_000_000, transcendentals=whole * channels
        ),
    )(place, convolved, params, reach_grad, reach_grad)
    keep_first, keep_rest = pl.pallas_call(
        keep_kernel,
        grid_spec=pltpu.PrefetchScalarGridSpec(
            num_scalar_prefetch=1,
            grid=(4,),
            in_specs=[
                pl.BlockSpec((whole, channels), lambda i, s: (0, 0)),
                pl.BlockSpec((utts, rows, block), column(0, 0)),
                pl.BlockSpec((utts, rows, block), column(1, 0)),
            ],
            out_specs=[
                pl.BlockSpec((2, block, block), early),
                pl.BlockSpec((2, block, block), late),
            ],
        ),
        out_shape=[jax.ShapeDtypeStruct((4, block, block), f32)] * 2,
        compiler_params=pltpu.CompilerParams(vmem_limit_bytes=24 << 20),
        cost_estimate=pl.CostEstimate(
            flops=whole * channels * channels, bytes_accessed=6_000_000, transcendentals=0
        ),
    )(place, active, reach_grad, reach_grad)
    return active, send_first, send_rest, keep_first, keep_rest


def pack_kernel(base, low, high, sums, out):
    groups, size = out.shape[0], out.shape[1] - 8
    first = pl.program_id(0) * groups
    total = base[...] + jnp.where(pl.program_id(0) < 2, low[...].astype(f32), high[...].astype(f32))
    filler = jnp.zeros((2, total.shape[1]), f32)
    for group in range(groups):
        row = first + group
        ride = jnp.concatenate([sums[pl.ds(row, 1), :], sums[pl.ds(32 + row, 1), :], sums[64:65, :]], 0)
        rounded = ride.astype(bf16).astype(f32)
        out[group] = jnp.concatenate(
            [total[group * size : (group + 1) * size], rounded, ride - rounded, filler], 0
        ).astype(bf16)


def packed(base, low, high, sums, count):
    half, block = base.shape
    size = half // count
    groups = count // 4
    by_rows = lambda i: (i, 0)
    return pl.pallas_call(
        pack_kernel,
        grid=(count // groups,),
        in_specs=[
            pl.BlockSpec((groups * size, block), by_rows),
            pl.BlockSpec((groups * size, block), lambda i: (jnp.minimum(i, 1), 0)),
            pl.BlockSpec((groups * size, block), lambda i: (jnp.maximum(i - 2, 0), 0)),
            pl.BlockSpec(sums.shape, lambda i: (0, 0)),
        ],
        out_specs=pl.BlockSpec((groups, size + 8, block), lambda i: (i, 0, 0)),
        out_shape=jax.ShapeDtypeStruct((count, size + 8, block), bf16),
        compiler_params=pltpu.CompilerParams(vmem_limit_bytes=16 << 20),
        cost_estimate=pl.CostEstimate(flops=2_000_000, bytes_accessed=4_000_000, transcendentals=0),
    )(base, low, high, sums)


def fill_padded(place, padded, before, own, after):
    utts, rows = own.shape[0], own.shape[1]
    for utt in range(utts):
        limit = limit_of(place, utt, utts, rows)
        padded[utt, 0:HALO, :] = masked_rows(before[utt], -HALO, limit)
        padded[utt, HALO : HALO + rows, :] = masked_rows(own[utt], 0, limit)
        if after is not None:
            padded[utt, HALO + rows :, :] = masked_rows(after[utt], rows, limit)


def correlate(padded, other, rows, store):
    for first in range(0, HALO, 8):
        running = [jnp.zeros((8, LANES), f32) for _ in range(8)]
        for utt in range(padded.shape[0]):
            for row in range(0, rows, 8):
                value = other[utt, row : row + 8, :]
                for tap in range(8):
                    at = row + first + tap + 1
                    running[tap] = running[tap] + padded[utt, at : at + 8, :] * value
        for tap in range(8):
            store(first + tap, jnp.sum(running[tap], axis=0, keepdims=True))


def early_kernel(place, before, own, convolved, stats, early, padded, centred):
    utts, rows = own.shape[0], own.shape[1]
    mean = stats[0, 0:1, :] / jnp.maximum(stats[0, 2:3, :], 1.0)
    fill_padded(place, padded, before, own, None)
    ones = jnp.zeros((HALO, LANES), f32)
    for utt in range(utts):
        limit = limit_of(place, utt, utts, rows)
        centred[utt] = masked_rows(convolved[utt] - mean, 0, limit)
        lag = (
            lax.broadcasted_iota(jnp.int32, (HALO, HALO + rows), 1)
            - lax.broadcasted_iota(jnp.int32, (HALO, HALO + rows), 0)
            - 1
        )
        band = jnp.where((lag >= 0) & (lag < jnp.minimum(limit, rows)), 1.0, 0.0).astype(bf16)
        ones = ones + jnp.dot(band, padded[utt].astype(bf16), preferred_element_type=f32)
    early[0:32, :] = ones

    def store(tap, value):
        early[32 + tap : 33 + tap, :] = value

    correlate(padded, centred, rows, store)


def early_sums(place, before, own, convolved, stats):
    utts, rows, channels = own.shape
    by_tile = lambda j, s: (0, 0, j)
    return pl.pallas_call(
        early_kernel,
        grid_spec=pltpu.PrefetchScalarGridSpec(
            num_scalar_prefetch=1,
            grid=(channels // LANES,),
            in_specs=[
                pl.BlockSpec((utts, HALO, LANES), by_tile),
                pl.BlockSpec((utts, rows, LANES), by_tile),
                pl.BlockSpec((utts, rows, LANES), by_tile),
                pl.BlockSpec((1, 3, LANES), stats_place(channels // 4 // LANES)),
            ],
            out_specs=pl.BlockSpec((64, LANES), lambda j, s: (0, j)),
            scratch_shapes=[
                pltpu.VMEM((utts, HALO + rows, LANES), f32),
                pltpu.VMEM((utts, rows, LANES), f32),
            ],
        ),
        out_shape=jax.ShapeDtypeStruct((64, channels), f32),
        compiler_params=pltpu.CompilerParams(vmem_limit_bytes=24 << 20),
        cost_estimate=pl.CostEstimate(flops=30_000_000, bytes_accessed=4_000_000, transcendentals=0),
    )(place, before, own, convolved, stats)


def late_kernel(
    place, params, before, own, convolved, act_grad, stats, early, sums, pre_out, normed_out, ends_out, padded, pre
):
    utts, rows = own.shape[0], own.shape[1]
    mean, inverse, gain, shift = (params[i : i + 1, :] for i in range(4))
    bias_sum = jnp.zeros((1, LANES), f32)
    gain_sum = jnp.zeros((1, LANES), f32)
    fill_padded(place, padded, before, own, None)
    for utt in range(utts):
        limit = limit_of(place, utt, utts, rows)
        for start in range(0, rows, 32):
            normed = (convolved[utt, start : start + 32, :] - mean) * inverse
            preact = normed * gain + shift
            sigmoid = jax.nn.sigmoid(preact)
            grad = act_grad[utt, start : start + 32, :] * sigmoid * (1.0 + preact * (1.0 - sigmoid))
            grad = masked_rows(grad, start, limit)
            normed = masked_rows(normed, start, limit)
            pre_out[utt, start : start + 32, :] = grad
            normed_out[utt, start : start + 32, :] = normed
            pre[utt, start : start + 32, :] = grad
            bias_sum = bias_sum + jnp.sum(grad, axis=0, keepdims=True)
            gain_sum = gain_sum + jnp.sum(grad * normed, axis=0, keepdims=True)
            if start == 0:
                ends_out[utt] = grad.astype(bf16)
                ends_out[utts + utt] = normed.astype(bf16)
    column = pl.program_id(0) // (pl.num_programs(0) // 4) >> 1
    near = (column - chip_of(place) & 3) >> 1

    def store(tap, value):
        sums[0, 0, near, tap : tap + 1, :] = value

    correlate(padded, pre, rows, store)
    ones = early[0:32, :]
    own_mean = stats[0, 0:1, :] / jnp.maximum(stats[0, 2:3, :], 1.0)
    sums[0, 0, near, 32:64, :] = ones
    sums[0, 0, near, 64:72, :] = jnp.zeros((8, LANES), f32) + bias_sum
    sums[0, 0, 1 - near, 0:32, :] = (early[32:64, :] + (own_mean - mean) * ones) * inverse
    sums[0, 0, 1 - near, 32:64, :] = jnp.zeros((32, LANES), f32)
    sums[0, 0, 1 - near, 64:72, :] = jnp.zeros((8, LANES), f32) + gain_sum


def late_sums(place, params, before, own, convolved, act_grad, stats, early):
    utts, rows, channels = own.shape
    block_tiles = channels // 4 // LANES

    def slot(j, s):
        column = j // block_tiles
        return ((column ^ s[9]) & 1, ((column >> 1) ^ (s[9] >> 1)) & 1, 0, 0, j % block_tiles)

    by_tile = lambda j, s: (0, 0, j)
    by_column = lambda j, s: (0, j)
    return pl.pallas_call(
        late_kernel,
        grid_spec=pltpu.PrefetchScalarGridSpec(
            num_scalar_prefetch=1,
            grid=(channels // LANES,),
            in_specs=[
                pl.BlockSpec((4, LANES), by_column),
                pl.BlockSpec((utts, HALO, LANES), by_tile),
                pl.BlockSpec((utts, rows, LANES), by_tile),
                pl.BlockSpec((utts, rows, LANES), by_tile),
                pl.BlockSpec((utts, rows, LANES), by_tile),
                pl.BlockSpec((1, 3, LANES), stats_place(block_tiles)),
                pl.BlockSpec((64, LANES), by_column),
            ],
            out_specs=[
                pl.BlockSpec((1, 1, 2, 72, LANES), slot),
                pl.BlockSpec((utts, rows, LANES), by_tile),
                pl.BlockSpec((utts, rows, LANES), by_tile),
                pl.BlockSpec((2 * utts, HALO, LANES), by_tile),
            ],
            scratch_shapes=[
                pltpu.VMEM((utts, HALO + rows, LANES), f32),
                pltpu.VMEM((utts, rows, LANES), f32),
            ],
        ),
        out_shape=[
            jax.ShapeDtypeStruct((2, 2, 2, 72, channels // 4), f32),
            jax.ShapeDtypeStruct((utts, rows, channels), f32),
            jax.ShapeDtypeStruct((utts, rows, channels), f32),
            jax.ShapeDtypeStruct((2 * utts, HALO, channels), bf16),
        ],
        compiler_params=pltpu.CompilerParams(vmem_limit_bytes=24 << 20),
        cost_estimate=pl.CostEstimate(flops=40_000_000, bytes_accessed=10_000_000, transcendentals=500_000),
    )(place, params, before, own, convolved, act_grad, stats, early)


def back_kernel(place, taps, params, pre, normed, ahead, out, grad):
    utts, rows = out.shape[0], out.shape[1]
    scale, bias_mean, gain_mean = (params[i : i + 1, :] for i in range(3))
    for utt in range(utts):
        limit = limit_of(place, utt, utts, rows)
        value = pre[utt] - bias_mean - normed[utt] * gain_mean
        grad[utt, 0:rows, :] = masked_rows(value * scale, 0, limit)
        value = ahead[utt].astype(f32) - bias_mean - ahead[utts + utt].astype(f32) * gain_mean
        grad[utt, rows:, :] = masked_rows(value * scale, rows, limit)
        for start in range(0, rows, 64):
            result = jnp.zeros((64, LANES), f32)
            for lead in range(HALO):
                tap = HALO - 1 - lead
                result = result + taps[tap : tap + 1, :] * grad[utt, start + lead : start + lead + 64, :]
            out[utt, start : start + 64, :] = masked_rows(result, start, limit).astype(bf16)


def frames_back(place, taps, params, pre, normed, ahead):
    utts, rows, channels = pre.shape
    by_tile = lambda j, s: (0, 0, j)
    return pl.pallas_call(
        back_kernel,
        grid_spec=pltpu.PrefetchScalarGridSpec(
            num_scalar_prefetch=1,
            grid=(channels // LANES,),
            in_specs=[
                pl.BlockSpec((HALO, LANES), lambda j, s: (0, j)),
                pl.BlockSpec((3, LANES), lambda j, s: (0, j)),
                pl.BlockSpec((utts, rows, LANES), by_tile),
                pl.BlockSpec((utts, rows, LANES), by_tile),
                pl.BlockSpec((2 * utts, HALO, LANES), by_tile),
            ],
            out_specs=pl.BlockSpec((utts, rows, LANES), by_tile),
            scratch_shapes=[pltpu.VMEM((utts, rows + HALO, LANES), f32)],
        ),
        out_shape=jax.ShapeDtypeStruct((utts, rows, channels), bf16),
        compiler_params=pltpu.CompilerParams(vmem_limit_bytes=24 << 20),
        cost_estimate=pl.CostEstimate(flops=30_000_000, bytes_accessed=5_000_000, transcendentals=0),
    )(place, taps, params, pre, normed, ahead)


def column_starts(place, block):
    chip, core = place[9] >> 1, place[9] & 1
    owners = (chip * 2 + core, (1 - chip) * 2 + core, chip * 2 + 1 - core, (1 - chip) * 2 + 1 - core)
    return [pl.multiple_of(owner * block, LANES) for owner in owners]


def act_kernel(place, grads, *refs):
    weights, out = refs[:-1], refs[-1]
    size, block = weights[1].shape
    utts, rows = grads.shape[0], grads.shape[1]
    columns = [
        jnp.concatenate([grads[utt, :, pl.ds(first, block)] for utt in range(utts)], 0)
        for first in column_starts(place, block)
    ]
    for half in range(2):
        for start in range(0, size, 384):
            part = slice(start, start + 384)
            whole = slice(half * size + start, half * size + start + 384)
            tiles = (weights[0][whole, :], weights[1 + half][part, :], weights[3][whole, :], weights[4 + half][part, :])
            total = jnp.zeros((utts * rows, 384), f32)
            for column, tile in zip(columns, tiles):
                total = total + lax.dot_general(
                    column, tile, (((1,), (1,)), ((), ())), preferred_element_type=f32
                )
            for utt in range(utts):
                out[utt, :, whole] = total[utt * rows : (utt + 1) * rows]


def mixed_kernel(place, active, *refs):
    weights, out = refs[:-1], refs[-1]
    size, block = weights[1].shape
    utts, rows = out.shape[0], out.shape[1]
    first, second = active[:, :size], active[:, size:]
    tiles = (
        (weights[0][:size, :], weights[0][size:, :]),
        (weights[1][...], weights[2][...]),
        (weights[3][:size, :], weights[3][size:, :]),
        (weights[4][...], weights[5][...]),
    )
    for column, (top, bottom) in zip(column_starts(place, block), tiles):
        total = jnp.dot(first, top, preferred_element_type=f32)
        total = total + jnp.dot(second, bottom, preferred_element_type=f32)
        total = total.astype(bf16)
        for utt in range(utts):
            out[utt, :, pl.ds(column, block)] = total[utt * rows : (utt + 1) * rows]


def with_weights(kernel, place, value, weights, shape, dtype):
    smem, vmem = pl.BlockSpec(memory_space=pltpu.SMEM), pl.BlockSpec(memory_space=pltpu.VMEM)
    return pl.pallas_call(
        kernel,
        in_specs=[smem] + [vmem] * (1 + len(weights)),
        out_specs=vmem,
        out_shape=jax.ShapeDtypeStruct(shape, dtype),
        compiler_params=pltpu.CompilerParams(vmem_limit_bytes=28 << 20),
        cost_estimate=pl.CostEstimate(flops=100_000_000, bytes_accessed=2_000_000, transcendentals=0),
    )(place, value, *weights)


def widen_kernel(place, value, *refs):
    refs[-1][0] = value[...].astype(f32)


def widened(place, value, other, whole):
    half, block = value.shape
    aliased = whole is not None
    return pl.pallas_call(
        widen_kernel,
        grid_spec=pltpu.PrefetchScalarGridSpec(
            num_scalar_prefetch=1,
            grid=(2,),
            in_specs=[pl.BlockSpec((half // 2, block), lambda i, s: (i, 0))]
            + [pl.BlockSpec(memory_space=pl.ANY)] * aliased,
            out_specs=pl.BlockSpec((1, half // 2, block), lambda i, s: ((s[8] & 1) ^ other, i, 0)),
        ),
        out_shape=jax.ShapeDtypeStruct((2, half, block), f32),
        input_output_aliases={2: 0} if aliased else {},
        compiler_params=pltpu.CompilerParams(vmem_limit_bytes=16 << 20),
        cost_estimate=pl.CostEstimate(flops=half * block, bytes_accessed=6 * half * block, transcendentals=0),
    )(place, value, *([whole] if aliased else []))


def moved(value, steps):
    count = lax.axis_size("tm")
    return lax.ppermute(value, "tm", [(i, i + steps) for i in range(count) if 0 <= i + steps < count])


def other_core(value):
    return lax.ppermute(value, "fsdp", [(0, 1), (1, 0), (2, 3), (3, 2)])


def other_chip(value):
    return lax.ppermute(value, "fsdp", [(0, 2), (2, 0), (1, 3), (3, 1)])


def across(value):
    return lax.ppermute(value, "tm", [(i, i ^ 1) for i in range(lax.axis_size("tm"))])


def along(value, steps):
    pairs = []
    for device in range(4 * lax.axis_size("tm")):
        plane, high, low, core = device // 8, device // 4 % 2, device // 2 % 2, device % 2
        place = (high * 2 + low + steps) % 4
        pairs.append((device, plane * 8 + place // 2 * 4 + place % 2 * 2 + core))
    return lax.ppermute(value, ("tm", "fsdp"), pairs)


def in_plane(value):
    count = lax.axis_size("tm")
    groups = [list(range(start, count, 2)) for start in range(2)]
    return lax.all_to_all(value, "tm", 0, 0, axis_index_groups=groups, tiled=True)


def from_all(value, chip, core):
    by_core = other_core(value)
    pair = jnp.where(core == 0, jnp.stack([value, by_core]), jnp.stack([by_core, value]))
    by_chip = other_chip(pair)
    return jnp.where(chip == 0, jnp.concatenate([pair, by_chip]), jnp.concatenate([by_chip, pair]))


def in_three(value):
    first = lax.reduce_precision(value, 8, 7)
    second = lax.reduce_precision(value - first, 8, 7)
    third = value - first - second
    return first.astype(bf16), second.astype(bf16), third.astype(bf16)


def on_device(frames_in, lengths, depth_kernel, norm_gain, norm_bias, out_weight, cotangent):
    utts, rows, channels = frames_in.shape
    tm, fsdp = lax.axis_index("tm"), lax.axis_index("fsdp")
    tm_count, fsdp_count = lax.axis_size("tm"), lax.axis_size("fsdp")
    block, half = channels // fsdp_count, channels // 2
    chip, core, high = fsdp // 2, fsdp % 2, tm % 2
    frames_valid = jnp.sum(lengths).astype(f32)
    table = [side for side, _ in QUARTERS] + [row for _, row in QUARTERS]
    scalars = jnp.concatenate(
        [lengths, jnp.stack([tm, fsdp]).astype(jnp.int32), jnp.array(table, jnp.int32)]
    )

    before = moved(frames_in[:, rows - HALO :, :], 1)
    convolved, stats = depthwise(scalars, depth_kernel, before, frames_in)

    plane = tm_count // 2
    chip_stats = in_vmem(pair_kernel, (3, half), stats, other_core(stats[1]))
    pieces = in_vmem(
        ring_kernel,
        (plane, 16, LANES),
        chip_stats,
        along(chip_stats, 1),
        along(chip_stats, -1),
        along(chip_stats, 2),
    )
    pieces, early_frames, columns, core_columns = lax.optimization_barrier(
        (pieces, frames_in, out_weight, other_core(out_weight))
    )
    pieces = in_plane(pieces)
    low_rows = along(columns[:half], 1)
    high_rows = along(columns[half:], -1)
    early = early_sums(scalars, before, early_frames, convolved, stats)
    pieces, early, low_rows, high_rows = lax.optimization_barrier((pieces, early, low_rows, high_rows))
    core_low, core_high = other_core(low_rows), other_core(high_rows)
    mine = in_vmem(moments_kernel, (2, half), lengths, pieces, scalars=1)
    params = in_vmem(
        params_kernel,
        (4, channels),
        scalars,
        mine,
        other_core(mine),
        norm_gain[None],
        norm_bias[None],
        scalars=1,
    )

    active, send_first, send_rest, keep_first, keep_rest = weight_terms(scalars, convolved, params, cotangent)
    send_first, core_low, core_high = lax.optimization_barrier((send_first, core_low, core_high))
    weights = (columns, low_rows, high_rows, core_columns, core_low, core_high)
    got_first, got_rest = other_core(send_first), other_core(send_rest)
    upward = (keep_first[:2] + got_first[:2].astype(f32)).astype(bf16)
    downward = (keep_first[2:] + got_first[2:].astype(f32)).astype(bf16)
    upward, downward, out_grads = lax.optimization_barrier((upward, downward, cotangent))
    below, above = along(upward, 1), along(downward, -1)
    act_grad = with_weights(act_kernel, scalars, out_grads, weights, frames_in.shape, f32)
    sums, pre, normed, first_rows = late_sums(
        scalars, params, before, frames_in, convolved, act_grad, stats, early
    )
    rest = keep_rest + got_rest.astype(f32)
    upward = (rest[0] + below[0].astype(f32)).astype(bf16)
    downward = (rest[1] + above[0].astype(f32)).astype(bf16)
    upward, downward, sums = lax.optimization_barrier((upward, downward, sums))
    near_sums = sums[0] + other_core(sums[1])
    base = jnp.concatenate([rest[2] + above[1].astype(f32), rest[3] + below[1].astype(f32)], 0)
    below, above = along(upward, 1), along(downward, -1)
    kept = (
        near_sums[0, 0]
        + along(near_sums[1, 0], 1)
        + along(near_sums[0, 1], 2)
        + along(near_sums[1, 1], -1)
    )

    outgoing = packed(base, below, above, kept, plane)
    incoming = in_plane(outgoing)
    summed = jnp.sum(incoming.astype(f32), axis=0)
    weight_rows = half // plane
    ride = summed[weight_rows : weight_rows + 3] + summed[weight_rows + 3 : weight_rows + 6]
    piece = summed[:weight_rows].astype(bf16)
    piece, ride, first_rows, active = lax.optimization_barrier((piece, ride, first_rows, active))
    ahead = moved(first_rows, -1)
    gathered = in_plane(jnp.broadcast_to(piece, (plane, *piece.shape)))
    mixed = with_weights(mixed_kernel, scalars, active, weights, frames_in.shape, bf16)
    gathered, ahead, mixed = lax.optimization_barrier((gathered, ahead, mixed))

    far_ride = across(ride)
    by_high = jnp.where(high == 0, jnp.stack([ride, far_ride]), jnp.stack([far_ride, ride]))
    ends = by_high[:, 2] / frames_valid
    gain_scale = lax.dynamic_slice_in_dim(norm_gain * params[1], fsdp * block, block, 0)
    kernel_own = gain_scale * (by_high[0, 0] - ends[0] * by_high[0, 1] - ends[1] * by_high[1, 0])
    rows_own = jnp.concatenate([by_high[:, 2], kernel_own[None]], 0)
    whole_rows = from_all(rows_own, chip, core).transpose(1, 0, 2).reshape(3, channels)
    bias_grad, gain_grad = whole_rows[0], whole_rows[1]
    back_params = jnp.concatenate([(norm_gain * params[1])[None], whole_rows[:2] / frames_valid], 0)
    frames_grad = frames_back(scalars, depth_kernel, back_params, pre, normed, ahead)

    mine = gathered.reshape(half, block)
    mine, kernel_row = lax.optimization_barrier((mine, whole_rows[2:]))
    theirs = across(mine)
    kernel_row = kernel_row.reshape(channels // LANES, LANES)
    kernel_row = jnp.concatenate([kernel_row, kernel_row[: 16 - channels // LANES]], 0)
    kernel_rows = in_plane(jnp.broadcast_to(kernel_row, (plane, 16, LANES)))
    kernel_grad = kernel_rows[:, : channels // LANES].reshape(plane, channels)
    weight_grad = widened(scalars, theirs, 1, widened(scalars, mine, 0, None)).reshape(channels, block)
    return (mixed, frames_grad, weight_grad, kernel_grad, gain_grad, bias_grad)


def solution(mesh):
    in_specs = (P("fsdp", "tm", None), P(), P(), P(), P(), P(None, "fsdp"), P("fsdp", "tm", None))
    out_specs = (P("fsdp", "tm", None), P("fsdp", "tm", None), P(None, "fsdp"), P(), P(), P())
    return jax.shard_map(
        on_device, mesh=mesh, in_specs=in_specs, out_specs=out_specs, check_vma=False
    )
```
